512 devices in a mesh: seq: 32 (over y_hi, x, core), section: 2 (over y_lo), tp: 8 (over z).
Axes of the slice: x: 4, y: 8 (y_hi: 4, y_lo: 2; y = y_hi * 2 + y_lo), z: 8, core: 2. Of those that a mesh axis runs over, the one named last changes fastest.
Arguments:
- hidden: bfloat16 [32, 3, 8192], P(None, None, 'seq'), may hold values from -1.796875 to 1.796875
- features: bfloat16 [32, 512, 8192], P('seq', ('section', 'tp')), may hold values from -6 to 6
- tiles: int32 [32], P('seq'), may hold values from 1 to 4, as said below
- key_value_weight: bfloat16 [2, 8192, 8, 256], P('section', 'seq', 'tp'), may hold values from -0.0625 to 0.0625
- k_gain: bfloat16 [2, 128], P('section'), may hold values from 1.5 to 2.5
- q_weight: bfloat16 [2, 8192, 8192], P('section', 'seq', 'tp'), may hold values from -0.0625 to 0.0625
- query_gain: bfloat16 [2, 128], P('section'), may hold values from 1.5 to 2.5
- o_weight: bfloat16 [2, 8192, 8192], P('section', 'tp', 'seq'), may hold values from -0.0625 to 0.0625
- attn_gate: float32 [2], P('section'), may hold values from 0.5 to 2
Outputs:
- key_cache: bfloat16 [2, 32, 512, 8, 128], P('section', 'seq', None, 'tp')
- value_cache: bfloat16 [2, 32, 512, 8, 128], P('section', 'seq', None, 'tp')
- section_out: bfloat16 [2, 32, 3, 8192], P('section', None, None, 'seq')
The draws below stay inside these ranges and needn't reach their ends.
Inputs may be any that keep to these rules, and one draw needn't show every extreme that they name: Request b's first tiles[b] * 128 image slots are valid. Some request has 4 tiles and some has 1.
All inputs are finite; a program needn't handle non-finite values.
Results may differ from the reference program's by a relative error of at most 0.025.
Values may be sent and summed in bfloat16 or wider, within the bound.
No kernel may reach another device: no remote copies, remote signals or barrier semaphores. Data moves between devices by JAX's collectives and lax.ppermute only.
A program may use at most 64 MiB of HBM per device.

```python
import math
import jax
import jax.numpy as jnp
from jax import lax

MODEL_WIDTH = 8192
QUERY_HEADS = 64
KEY_VALUE_HEADS = 8
HEAD_WIDTH = 128
TILES_MAX = 4
TILE_TOK = 128
STEPS = 3
REQUEST_TOTAL = 32
IMAGE_SLOTS = 512
N_SECTION = 2


def draw_tiles(key, part):
    key = jax.random.fold_in(key, 11)
    first_key, second_key, third_key = jax.random.split(key, 3)
    counts = jax.random.randint(first_key, (REQUEST_TOTAL,), 1, TILES_MAX + 1)
    highest = jax.random.randint(second_key, (), 0, REQUEST_TOTAL)
    lowest = (highest + jax.random.randint(third_key, (), 1, REQUEST_TOTAL)) % REQUEST_TOTAL
    counts = counts.at[highest].set(TILES_MAX)
    counts = counts.at[lowest].set(1)
    return counts.astype(jnp.int32)


def spiked(result, key, source, target, shards_of, factor):
    def block_of(axis_at):
        return (jnp.arange(result.shape[axis_at]) // (result.shape[axis_at] // shards_of)).reshape((-1,) + (1,) * (result.ndim - 1 - axis_at))

    first = jax.random.permutation(key, shards_of)[block_of(target)]
    second = (block_of(target) + shards_of // 2) % shards_of
    return jnp.where((block_of(source) == first) | (block_of(source) == second), factor * result, result)


def shard_levels(own_key, extent, shards, low, largest):
    factor_of, own = 1.0, jax.random.fold_in(own_key, 6)
    for axis_at, shards_of in shards:
        steps = jnp.exp(jax.random.uniform(jax.random.fold_in(own, axis_at), (shards_of,), jnp.float32, low / len(shards), largest / len(shards)))
        factor_of = factor_of * jnp.repeat(steps, extent[axis_at] // shards_of).reshape([-1 if axis == axis_at else 1 for axis in range(len(extent))])
    return factor_of


def gaussian(rng, shape, scale, reach, shards=(), kind=jnp.bfloat16):
    entries = jax.random.normal(rng, shape, jnp.float32) * scale
    if len(shards) > 0:
        entries = shard_levels(rng, shape, shards, -0.22, 0.18) * entries
    return jnp.clip(entries, min=-reach, max=reach).astype(kind)


def bell_draw_with(own_key, extent, scale, reach, cuts, heavy, held_as=jnp.bfloat16):
    array = scale * jax.random.normal(own_key, extent, jnp.float32)
    if cuts:
        array = array * shard_levels(own_key, extent, cuts, -0.22, 0.18)
    return jnp.clip(spiked(array, jax.random.fold_in(own_key, 3), *heavy), -reach, reach).astype(held_as)


def setup_inputs(seed: int = 0) -> dict:
    splits = jax.random.split(jax.random.key(seed), 10)
    return {
        "hidden": bell_draw_with(splits[0], (REQUEST_TOTAL, STEPS, MODEL_WIDTH), 0.3, 1.796875, ((2, 32),), (2, 0, 32, 2.75)),
        "features": gaussian(splits[1], (REQUEST_TOTAL, IMAGE_SLOTS, MODEL_WIDTH), 1.0, 6.0, ((0, 32), (1, 16))),
        "tiles": draw_tiles(jax.random.fold_in(splits[9], 71), 0),
        "key_value_weight": gaussian(splits[3], (N_SECTION, MODEL_WIDTH, KEY_VALUE_HEADS, 2 * HEAD_WIDTH), MODEL_WIDTH ** -0.5, 0.0625, ((0, 2), (1, 32), (2, 8))),
        "k_gain": jnp.clip(jnp.exp(math.log(2.5) - 0.51082562 * jax.random.uniform(splits[4], (N_SECTION, HEAD_WIDTH), jnp.float32) ** shard_levels(splits[4], (N_SECTION, HEAD_WIDTH), ((0, 2),), -0.2, 0.2)), 1.5, 2.5).astype(jnp.bfloat16),
        "q_weight": gaussian(splits[5], (N_SECTION, MODEL_WIDTH, QUERY_HEADS * HEAD_WIDTH), MODEL_WIDTH ** -0.5, 0.0625, ((0, 2), (1, 32), (2, 8))),
        "query_gain": jnp.clip(jnp.exp(math.log(2.5) - 0.51082562 * jax.random.uniform(splits[6], (N_SECTION, HEAD_WIDTH), jnp.float32) ** shard_levels(splits[6], (N_SECTION, HEAD_WIDTH), ((0, 2),), -0.2, 0.2)), 1.5, 2.5).astype(jnp.bfloat16),
        "o_weight": gaussian(splits[7], (N_SECTION, QUERY_HEADS * HEAD_WIDTH, MODEL_WIDTH), (QUERY_HEADS * HEAD_WIDTH) ** -0.5, 0.0625, ((0, 2), (1, 8), (2, 32))),
        "attn_gate": jnp.clip(0.5 + 1.5 * jax.random.uniform(splits[8], (N_SECTION,), jnp.float32) ** shard_levels(splits[8], (N_SECTION,), ((0, 2),), -0.2, 0.2), 0.5, 2.0),
    }


def norm_per_head(values, gain):
    values = values.astype(jnp.float32)
    factor = lax.rsqrt(lax.optimization_barrier(jnp.mean(values * values, axis=-1, keepdims=True)) + 1e-05)
    return values * factor * gain.astype(jnp.float32)

def build_cache(features, weight_matrix, gain):
    rows_of_tokens = features.reshape(REQUEST_TOTAL * IMAGE_SLOTS, MODEL_WIDTH)
    projected_rows = jnp.dot(rows_of_tokens, weight_matrix.reshape(MODEL_WIDTH, KEY_VALUE_HEADS * 2 * HEAD_WIDTH), preferred_element_type=jnp.float32)
    projected_rows = projected_rows.reshape(REQUEST_TOTAL, IMAGE_SLOTS, KEY_VALUE_HEADS, 2 * HEAD_WIDTH)
    keys = norm_per_head(projected_rows[..., :HEAD_WIDTH], gain).astype(jnp.bfloat16)
    return (keys, projected_rows[..., HEAD_WIDTH:].astype(jnp.bfloat16))

def cross_layer(state, keys, values, live, q_weight, query_gain, o_weight, gate):
    token_positions = state.shape[1]
    query_vector = jnp.dot(state.reshape(-1, MODEL_WIDTH), q_weight, preferred_element_type=jnp.float32)
    query_vector = norm_per_head(query_vector.reshape(REQUEST_TOTAL, token_positions, KEY_VALUE_HEADS, QUERY_HEADS // KEY_VALUE_HEADS, HEAD_WIDTH), query_gain).astype(jnp.bfloat16)
    scores = jnp.einsum('bsgqd,blgd->bsgql', query_vector.astype(jnp.float32), keys.astype(jnp.float32)) / math.sqrt(HEAD_WIDTH)
    weights = jnp.where(live[:, None, None, None, :], jnp.exp(scores), 0.0)
    weights = (weights / lax.optimization_barrier(jnp.sum(weights, axis=-1, keepdims=True))).astype(jnp.bfloat16)
    attended = jnp.einsum('bsgql,blgd->bsgqd', weights.astype(jnp.float32), values.astype(jnp.float32)).astype(jnp.bfloat16)
    mixed = jnp.dot(attended.reshape(-1, QUERY_HEADS * HEAD_WIDTH), o_weight, preferred_element_type=jnp.float32)
    return (state.astype(jnp.float32) + jnp.tanh(gate) * mixed.reshape(state.shape)).astype(jnp.bfloat16)

def reference(hidden, features, tiles, key_value_weight, k_gain, q_weight, query_gain, o_weight, attn_gate):
    live = jnp.arange(IMAGE_SLOTS, dtype=jnp.int32)[None, :] < (tiles * TILE_TOK)[:, None]
    key_list = []
    value_list = []
    out_list = []
    state = hidden
    for layer_index in range(N_SECTION):
        keys, values = build_cache(features, key_value_weight[layer_index], k_gain[layer_index])
        state = cross_layer(state, keys, values, live, q_weight[layer_index], query_gain[layer_index], o_weight[layer_index], attn_gate[layer_index])
        key_list.append(keys)
        value_list.append(values)
        out_list.append(state)
    return (jnp.stack(key_list), jnp.stack(value_list), jnp.stack(out_list))
```

```python
import math

import jax
import jax.numpy as jnp
from jax import lax
from jax.sharding import Mesh, PartitionSpec as P

TILE_TOK = 128
SEQ = ("far", "row", "core")
BF16 = jnp.bfloat16
F32 = jnp.float32


def norm_per_head(values, gain):
    factor = lax.rsqrt(jnp.mean(values * values, axis=-1, keepdims=True) + 1e-05)
    return values * factor * gain.astype(F32)


def exchange(blocks, axis):
    return lax.all_to_all(blocks, axis, 0, 0, tiled=True)


def gathered(block, axis):
    return exchange(jnp.broadcast_to(block[None], (lax.axis_size(axis),) + block.shape), axis)


def gather_weight(weight):
    rows, columns = weight.shape
    by_far = gathered(weight, "far")
    by_row = gathered(by_far, "row")
    by_core = gathered(by_row, "core")
    return jnp.transpose(by_core, (2, 1, 0, 3, 4)).reshape(-1, columns)


def layer(state, weight, query_gain, keys, values, live, output_weight, gate):
    requests, positions, width = state.shape
    head_size = keys.shape[1]
    group = weight.shape[1] // head_size
    partial_query = jnp.dot(
        state.reshape(-1, width), weight, preferred_element_type=F32
    ).astype(BF16)
    pieces = exchange(partial_query.reshape(requests, positions, group * head_size), SEQ)
    query = jnp.sum(pieces.astype(F32), axis=0).reshape(positions * group, head_size)
    query = norm_per_head(query, query_gain).astype(BF16)
    scores = jnp.dot(query, keys.T, preferred_element_type=F32) / math.sqrt(head_size)
    weights = jnp.where(live, jnp.exp(scores), 0.0)
    weights = (weights / jnp.sum(weights, axis=-1, keepdims=True)).astype(BF16)
    attended = jnp.dot(weights, values, preferred_element_type=F32).astype(BF16)
    everyone = gathered(attended.reshape(positions, group * head_size), SEQ)
    partial_out = jnp.dot(
        everyone.reshape(requests * positions, -1), output_weight, preferred_element_type=F32
    )
    return (gate * partial_out).astype(BF16)


def body(
    hidden, features, tiles, key_value_weight, k_gain, q_weight, query_gain, o_weight, attn_gate
):
    head_size = k_gain.shape[1]
    section_index = lax.axis_index("section")
    tensor_count = lax.axis_size("tp")
    gate = jnp.tanh(attn_gate[0])

    tokens = lax.all_gather(features[0], ("section", "tp"), axis=0, tiled=True)
    full_weight = gather_weight(key_value_weight[0, :, 0, :])
    projected = jnp.dot(tokens, full_weight, preferred_element_type=F32)
    keys = norm_per_head(projected[:, :head_size], k_gain[0]).astype(BF16)
    values = projected[:, head_size:].astype(BF16)
    live = jnp.arange(keys.shape[0], dtype=jnp.int32)[None, :] < tiles[0] * TILE_TOK

    def step(state):
        return layer(
            state, q_weight[0], query_gain[0], keys, values, live, o_weight[0], gate
        )

    def added(state, pieces):
        total = jnp.sum(pieces.astype(F32), axis=0).reshape(state.shape)
        return (state.astype(F32) + total).astype(BF16)

    everywhere = gathered(step(hidden), ("section", "tp"))
    first = added(hidden, everywhere[:tensor_count])
    second = added(first, gathered(step(first), "tp"))
    section_out = jnp.where(section_index == 0, first, second)
    return (keys[None, None, :, None, :], values[None, None, :, None, :], section_out[None])


def solution(mesh):
    devices = mesh.devices
    fine = Mesh(
        devices.reshape(4, 4, 2, devices.shape[1], devices.shape[2]),
        ("far", "row", "core", "section", "tp"),
    )
    return jax.shard_map(
        body,
        mesh=fine,
        in_specs=(
            P(None, None, SEQ),
            P(SEQ, ("section", "tp"), None),
            P(SEQ),
            P("section", SEQ, "tp", None),
            P("section", None),
            P("section", SEQ, "tp"),
            P("section", None),
            P("section", "tp", SEQ),
            P("section"),
        ),
        out_specs=(
            P("section", SEQ, None, "tp", None),
            P("section", SEQ, None, "tp", None),
            P("section", None, None, SEQ),
        ),
        check_vma=False,
    )
```

```python
import math

import jax
import jax.numpy as jnp
from jax import lax
from jax.sharding import Mesh, PartitionSpec as P

TILE_TOK = 128
SEQ = ("far", "row", "core")
BF16 = jnp.bfloat16
F32 = jnp.float32


def norm_per_head(values, gain):
    factor = lax.rsqrt(jnp.mean(values * values, axis=-1, keepdims=True) + 1e-05)
    return values * factor * gain.astype(F32)


def exchange(blocks, axis):
    return lax.all_to_all(blocks, axis, 0, 0, tiled=True)


def gathered(block, axis):
    return exchange(jnp.broadcast_to(block[None], (lax.axis_size(axis),) + block.shape), axis)


def after(value, *earlier):
    return lax.optimization_barrier((value, *earlier))[0]


def to_query(state, weight):
    requests, positions, width = state.shape
    partial_query = jnp.dot(
        state.reshape(-1, width), weight, preferred_element_type=F32
    ).astype(BF16)
    pieces = exchange(partial_query.reshape(requests, positions, -1), SEQ)
    return jnp.sum(pieces.astype(F32), axis=0)


def attend(query, query_gain, keys, values, live, output_weight, gate):
    positions = query.shape[0]
    head_size = keys.shape[1]
    query = norm_per_head(query.reshape(-1, head_size), query_gain).astype(BF16)
    scores = jnp.dot(query, keys.T, preferred_element_type=F32) / math.sqrt(head_size)
    weights = jnp.where(live, jnp.exp(scores), 0.0)
    weights = (weights / jnp.sum(weights, axis=-1, keepdims=True)).astype(BF16)
    attended = jnp.dot(weights, values, preferred_element_type=F32).astype(BF16)
    everyone = gathered(attended.reshape(positions, -1), SEQ)
    partial_out = jnp.dot(
        everyone.reshape(-1, output_weight.shape[0]), output_weight, preferred_element_type=F32
    )
    return (gate * partial_out).astype(BF16)


def body(
    hidden, features, tiles, key_value_weight, k_gain, q_weight, query_gain, o_weight, attn_gate
):
    head_size = k_gain.shape[1]
    section = lax.axis_index("section")
    tensor_count = lax.axis_size("tp")
    fars, rows, cores = (lax.axis_size(name) for name in SEQ)
    gate = jnp.tanh(attn_gate[0])

    tokens = features.shape[1]
    halves = features.reshape(tokens, fars * rows, cores, -1)
    first_half = halves[:, :, 0].reshape(tokens, -1)
    second_half = halves[:, :, 1].reshape(tokens, -1)
    kept = jnp.where(section == 0, first_half, second_half)
    given = jnp.where(section == 0, second_half, first_half)
    received = lax.ppermute(given, "section", [(0, 1), (1, 0)])
    pair = jnp.where(
        section == 0,
        jnp.stack([kept, received]),
        jnp.stack([received, kept]),
    ).reshape(2 * tokens, -1)

    own_weight = key_value_weight[0, :, 0, :]
    columns = own_weight.shape[1]
    part_rows = own_weight.shape[0] // cores
    parts = jnp.broadcast_to(
        own_weight.reshape(1, cores, part_rows, columns), (2, cores, part_rows, columns)
    )
    parts = exchange(parts.reshape(2 * cores, part_rows, columns), ("section", "core"))
    parts = parts.reshape(2, cores, part_rows, columns)
    parts = jnp.where(section == 0, parts[:, 0], parts[:, 1])
    first_part, second_part = parts[0], parts[1]

    gathered_tokens = lax.all_gather(pair, "tp", axis=0, tiled=True)
    by_core = gathered(gathered(gathered(first_part, "far"), "row"), "core")
    first_weight = jnp.transpose(by_core, (2, 1, 0, 3, 4)).reshape(-1, columns)
    first_query = to_query(after(hidden, by_core), q_weight[0])

    def projected(weight):
        return jnp.dot(gathered_tokens, weight, preferred_element_type=F32)

    def handed(partial_sum, direction):
        return lax.ppermute(partial_sum.astype(BF16), "section", [direction])

    def cache(partial_sum, other):
        total = partial_sum + other.astype(F32)
        keys = norm_per_head(total[:, :head_size], k_gain[0]).astype(BF16)
        return keys, total[:, head_size:].astype(BF16)

    def added(state, pieces):
        total = jnp.sum(pieces.astype(F32), axis=0).reshape(state.shape)
        return (state.astype(F32) + total).astype(BF16)

    slots = jnp.arange(2 * tensor_count * tokens, dtype=jnp.int32)
    place = slots // tokens
    slots = (place % 2 * tensor_count + place // 2) * tokens + slots % tokens
    live = slots[None, :] < tiles[0] * TILE_TOK

    first_partial = projected(first_weight)
    first_keys, first_values = cache(first_partial, handed(first_partial, (1, 0)))
    second_weight = lax.all_gather(
        after(second_part, gathered_tokens), SEQ, axis=0, tiled=True
    )
    first_sum = attend(
        first_query, query_gain[0], first_keys, first_values, live, o_weight[0], gate
    )
    everywhere = gathered(first_sum, ("section", "tp"))
    second_partial = projected(after(second_weight, first_sum))
    second_other = handed(second_partial, (0, 1))
    first = added(hidden, everywhere[:tensor_count])
    second_query = to_query(after(first, second_partial), q_weight[0])
    second_keys, second_values = cache(second_partial, second_other)
    second_sum = attend(
        second_query, query_gain[0], second_keys, second_values, live, o_weight[0], gate
    )
    second = added(first, gathered(second_sum, "tp"))

    def placed(ours, theirs):
        chosen = jnp.where(section == 0, ours, theirs)
        chosen = chosen.reshape(tensor_count, 2, tokens, head_size)
        return jnp.transpose(chosen, (1, 0, 2, 3)).reshape(1, 1, -1, 1, head_size)

    keys = placed(first_keys, second_keys)
    values = placed(first_values, second_values)
    section_out = jnp.where(section == 0, first, second)
    return (keys, values, section_out[None])


def solution(mesh):
    devices = mesh.devices
    fine = Mesh(
        devices.reshape(4, 4, 2, devices.shape[1], devices.shape[2]),
        ("far", "row", "core", "section", "tp"),
    )
    return jax.shard_map(
        body,
        mesh=fine,
        in_specs=(
            P(None, None, SEQ),
            P(SEQ, ("section", "tp"), None),
            P(SEQ),
            P("section", SEQ, "tp", None),
            P("section", None),
            P("section", SEQ, "tp"),
            P("section", None),
            P("section", "tp", SEQ),
            P("section"),
        ),
        out_specs=(
            P("section", SEQ, None, "tp", None),
            P("section", SEQ, None, "tp", None),
            P("section", None, None, SEQ),
        ),
        check_vma=False,
    )
```

```python
import math

import jax
import jax.numpy as jnp
from jax import lax
from jax.experimental import pallas as pl
from jax.experimental.pallas import tpu as pltpu
from jax.sharding import Mesh, PartitionSpec as P

TILE_TOK = 128
SEQ = ("far", "row", "core")
BF16 = jnp.bfloat16
F32 = jnp.float32


def norm_per_head(values, gain):
    factor = lax.rsqrt(jnp.mean(values * values, axis=-1, keepdims=True) + 1e-05)
    return values * factor * gain.astype(F32)


def exchange(blocks, axis):
    return lax.all_to_all(blocks, axis, 0, 0, tiled=True)


def gathered(block, axis):
    return exchange(jnp.broadcast_to(block[None], (lax.axis_size(axis),) + block.shape), axis)


def after(value, *earlier):
    return lax.optimization_barrier((value, *earlier))[0]


def halved(rows, run):
    count, width = rows.shape

    def deal(rows_ref, halves_ref):
        for column in range(0, width, 2 * run):
            to = pl.ds(column // 2, run)
            halves_ref[0, :, to] = rows_ref[:, pl.ds(column, run)]
            halves_ref[1, :, to] = rows_ref[:, pl.ds(column + run, run)]

    return pl.pallas_call(
        deal,
        out_shape=jax.ShapeDtypeStruct((2, count, width // 2), rows.dtype),
        in_specs=[pl.BlockSpec(memory_space=pltpu.VMEM)],
        out_specs=pl.BlockSpec(memory_space=pltpu.VMEM),
        compiler_params=pltpu.CompilerParams(vmem_limit_bytes=4 * 1024 * 1024),
        cost_estimate=pl.CostEstimate(
            flops=0, bytes_accessed=4 * count * width, transcendentals=0
        ),
        name="deal_halves",
    )(rows)


def to_query(state, weight):
    requests, positions, width = state.shape
    partial_query = jnp.dot(
        state.reshape(-1, width), weight, preferred_element_type=F32
    ).astype(BF16)
    pieces = exchange(partial_query.reshape(requests, positions, -1), SEQ)
    return jnp.sum(pieces.astype(F32), axis=0)


def attend(query, query_gain, keys, values, live, output_weight, gate):
    positions = query.shape[0]
    head_size = keys.shape[1]
    query = norm_per_head(query.reshape(-1, head_size), query_gain).astype(BF16)
    scores = jnp.dot(query, keys.T, preferred_element_type=F32) / math.sqrt(head_size)
    weights = jnp.where(live, jnp.exp(scores), 0.0)
    weights = (weights / jnp.sum(weights, axis=-1, keepdims=True)).astype(BF16)
    attended = jnp.dot(weights, values, preferred_element_type=F32).astype(BF16)
    everyone = gathered(attended.reshape(positions, -1), SEQ)
    partial_out = jnp.dot(
        everyone.reshape(-1, output_weight.shape[0]), output_weight, preferred_element_type=F32
    )
    return (gate * partial_out).astype(BF16)


def body(
    hidden, features, tiles, key_value_weight, k_gain, q_weight, query_gain, o_weight, attn_gate
):
    head_size = k_gain.shape[1]
    section = lax.axis_index("section")
    tensor_count = lax.axis_size("tp")
    fars, rows, cores = (lax.axis_size(name) for name in SEQ)
    gate = jnp.tanh(attn_gate[0])

    tokens, width = features.shape[1:]
    run = width // (fars * rows * cores * 2)
    pair = exchange(halved(features[0], run), "section").reshape(2 * tokens, -1)

    own_weight = key_value_weight[0, :, 0, :]
    columns = own_weight.shape[1]
    parts = exchange(after(own_weight, pair).reshape(2, run, columns), "section")
    first_part, second_part = parts[0], parts[1]

    gathered_tokens = lax.all_gather(pair, "tp", axis=0, tiled=True)
    by_core = gathered(gathered(gathered(first_part, "far"), "row"), "core")
    first_weight = jnp.transpose(by_core, (2, 1, 0, 3, 4)).reshape(-1, columns)
    first_query = to_query(after(hidden, by_core), q_weight[0])

    def projected(weight):
        return jnp.dot(gathered_tokens, weight, preferred_element_type=F32)

    def handed(partial_sum, direction):
        return lax.ppermute(partial_sum.astype(BF16), "section", [direction])

    def cache(partial_sum, other):
        total = partial_sum + other.astype(F32)
        keys = norm_per_head(total[:, :head_size], k_gain[0]).astype(BF16)
        return keys, total[:, head_size:].astype(BF16)

    def added(state, total):
        return (state.astype(F32) + total.reshape(state.shape)).astype(BF16)

    slots = jnp.arange(2 * tensor_count * tokens, dtype=jnp.int32)
    place = slots // tokens
    slots = (place % 2 * tensor_count + place // 2) * tokens + slots % tokens
    live = slots[None, :] < tiles[0] * TILE_TOK

    first_partial = projected(first_weight)
    first_keys, first_values = cache(first_partial, handed(first_partial, (1, 0)))
    second_weight = lax.all_gather(
        after(second_part, gathered_tokens), SEQ, axis=0, tiled=True
    )
    first_sum = attend(
        first_query, query_gain[0], first_keys, first_values, live, o_weight[0], gate
    )
    first_sum = first_sum.reshape(tensor_count, -1, first_sum.shape[1])
    summed = jnp.sum(exchange(first_sum, "tp").astype(F32), axis=0).astype(BF16)
    first = added(hidden, gathered(summed, ("section", "tp"))[:tensor_count].astype(F32))
    second_partial = projected(after(second_weight, first))
    second_other = handed(second_partial, (0, 1))
    second_query = to_query(first, q_weight[0])
    second_keys, second_values = cache(second_partial, second_other)
    second_sum = attend(
        second_query, query_gain[0], second_keys, second_values, live, o_weight[0], gate
    )
    second = added(first, jnp.sum(gathered(second_sum, "tp").astype(F32), axis=0))

    def placed(ours, theirs):
        chosen = jnp.where(section == 0, ours, theirs)
        chosen = chosen.reshape(tensor_count, 2, tokens, head_size)
        return jnp.transpose(chosen, (1, 0, 2, 3)).reshape(1, 1, -1, 1, head_size)

    keys = placed(first_keys, second_keys)
    values = placed(first_values, second_values)
    section_out = jnp.where(section == 0, first, second)
    return (keys, values, section_out[None])


def solution(mesh):
    devices = mesh.devices
    fine = Mesh(
        devices.reshape(4, 4, 2, devices.shape[1], devices.shape[2]),
        ("far", "row", "core", "section", "tp"),
    )
    return jax.shard_map(
        body,
        mesh=fine,
        in_specs=(
            P(None, None, SEQ),
            P(SEQ, ("section", "tp"), None),
            P(SEQ),
            P("section", SEQ, "tp", None),
            P("section", None),
            P("section", SEQ, "tp"),
            P("section", None),
            P("section", "tp", SEQ),
            P("section"),
        ),
        out_specs=(
            P("section", SEQ, None, "tp", None),
            P("section", SEQ, None, "tp", None),
            P("section", None, None, SEQ),
        ),
        check_vma=False,
    )
```

```python
import math

import jax
import jax.numpy as jnp
from jax import lax
from jax.experimental import pallas as pl
from jax.experimental.pallas import tpu as pltpu
from jax.sharding import Mesh, PartitionSpec as P

TILE_TOK = 128
SEQ = ("far", "row", "core")
BF16 = jnp.bfloat16
F32 = jnp.float32


def norm_per_head(values, gain):
    factor = lax.rsqrt(jnp.mean(values * values, axis=-1, keepdims=True) + 1e-05)
    return values * factor * gain.astype(F32)


def exchange(blocks, axis):
    return lax.all_to_all(blocks, axis, 0, 0, tiled=True)


def gathered(block, axis):
    return exchange(jnp.broadcast_to(block[None], (lax.axis_size(axis),) + block.shape), axis)


def after(value, *earlier):
    return lax.optimization_barrier((value, *earlier))[0]


def dealt(rows, weight, section):
    count, width = rows.shape
    run = weight.shape[0] // 2
    columns = weight.shape[1]

    def deal(section_ref, rows_ref, weight_ref, kept_ref, given_ref, kept_weight_ref, given_weight_ref):
        def split(first_ref, second_ref, first_weight_ref, second_weight_ref):
            for column in range(0, width, 2 * run):
                to = pl.ds(column // 2, run)
                first_ref[:, to] = rows_ref[:, pl.ds(column, run)]
                second_ref[:, to] = rows_ref[:, pl.ds(column + run, run)]
            first_weight_ref[...] = weight_ref[pl.ds(0, run), :]
            second_weight_ref[...] = weight_ref[pl.ds(run, run), :]

        @pl.when(section_ref[0] == 0)
        def _():
            split(kept_ref, given_ref, kept_weight_ref, given_weight_ref)

        @pl.when(section_ref[0] != 0)
        def _():
            split(given_ref, kept_ref, given_weight_ref, kept_weight_ref)

    half = jax.ShapeDtypeStruct((count, width // 2), rows.dtype)
    half_weight = jax.ShapeDtypeStruct((run, columns), weight.dtype)
    vmem = pl.BlockSpec(memory_space=pltpu.VMEM)
    return pl.pallas_call(
        deal,
        out_shape=(half, half, half_weight, half_weight),
        in_specs=[pl.BlockSpec(memory_space=pltpu.SMEM), vmem, vmem],
        out_specs=(vmem, vmem, vmem, vmem),
        compiler_params=pltpu.CompilerParams(vmem_limit_bytes=4 * 1024 * 1024),
        cost_estimate=pl.CostEstimate(
            flops=0, bytes_accessed=4 * count * width, transcendentals=0
        ),
        name="deal_halves",
    )(section.reshape(1), rows, weight)


def to_query(state, weight):
    requests, positions, width = state.shape
    partial_query = jnp.dot(
        state.reshape(-1, width), weight, preferred_element_type=F32
    ).astype(BF16)
    pieces = exchange(partial_query.reshape(requests, positions, -1), SEQ)
    return jnp.sum(pieces.astype(F32), axis=0)


def attend(query, query_gain, keys, values, live, output_weight, gate):
    positions = query.shape[0]
    head_size = keys.shape[1]
    query = norm_per_head(query.reshape(-1, head_size), query_gain).astype(BF16)
    scores = jnp.dot(query, keys.T, preferred_element_type=F32) / math.sqrt(head_size)
    weights = jnp.where(live, jnp.exp(scores), 0.0)
    weights = (weights / jnp.sum(weights, axis=-1, keepdims=True)).astype(BF16)
    attended = jnp.dot(weights, values, preferred_element_type=F32).astype(BF16)
    everyone = gathered(attended.reshape(positions, -1), SEQ)
    partial_out = jnp.dot(
        everyone.reshape(-1, output_weight.shape[0]), output_weight, preferred_element_type=F32
    )
    return (gate * partial_out).astype(BF16)


def body(
    hidden, features, tiles, key_value_weight, k_gain, q_weight, query_gain, o_weight, attn_gate
):
    head_size = k_gain.shape[1]
    section = lax.axis_index("section")
    tensor_count = lax.axis_size("tp")
    fars, rows, cores = (lax.axis_size(name) for name in SEQ)
    gate = jnp.tanh(attn_gate[0])

    tokens = features.shape[1]
    swap = [(0, 1), (1, 0)]
    kept, given, kept_weight, given_weight = dealt(
        features[0], key_value_weight[0, :, 0, :], section.astype(jnp.int32)
    )
    columns = kept_weight.shape[1]
    near_tokens = lax.all_gather(kept, "tp", axis=0, tiled=True)
    got_weight = lax.ppermute(given_weight, "section", swap)
    got = lax.ppermute(after(given, given_weight), "section", swap)
    far_tokens = lax.all_gather(got, "tp", axis=0, tiled=True)
    first_part = jnp.where(section == 0, kept_weight, got_weight)
    second_part = jnp.where(section == 0, got_weight, kept_weight)
    by_far = gathered(first_part, "far")
    by_core = gathered(gathered(after(by_far, got), "row"), "core")
    first_weight = jnp.transpose(by_core, (2, 1, 0, 3, 4)).reshape(-1, columns)

    def projected(rows, weight):
        return jnp.dot(rows, weight, preferred_element_type=F32)

    def handed(partial_sum, direction):
        return lax.ppermute(partial_sum, "section", [direction]).astype(F32)

    def cache(total):
        keys = norm_per_head(total[:, :head_size], k_gain[0]).astype(BF16)
        return keys, total[:, head_size:].astype(BF16)

    def added(state, total):
        return (state.astype(F32) + total.reshape(state.shape)).astype(BF16)

    slots = jnp.arange(2 * tensor_count * tokens, dtype=jnp.int32)
    slots = (slots + section * tensor_count * tokens) % slots.shape[0]
    live = slots[None, :] < tiles[0] * TILE_TOK

    first_near = projected(near_tokens, first_weight)
    given_near, early_hidden = lax.optimization_barrier((first_near.astype(BF16), hidden))
    for_far = handed(given_near, (1, 0))
    first_query = to_query(early_hidden, q_weight[0])
    first_far = projected(after(far_tokens, first_query), first_weight)
    for_near = handed(first_far.astype(BF16), (1, 0))
    first_keys, first_values = cache(
        jnp.concatenate([first_near + for_near, first_far + for_far])
    )
    second_weight = lax.all_gather(
        after(second_part, far_tokens), SEQ, axis=0, tiled=True
    )
    first_sum = attend(
        first_query, query_gain[0], first_keys, first_values, live, o_weight[0], gate
    )
    first_sum = first_sum.reshape(tensor_count, -1, first_sum.shape[1])
    summed = jnp.sum(exchange(first_sum, "tp").astype(F32), axis=0).astype(BF16)
    first = added(hidden, gathered(summed, ("section", "tp"))[:tensor_count].astype(F32))
    second_weight = after(second_weight, first)
    second_near = projected(near_tokens, second_weight)
    second_far = projected(far_tokens, second_weight)
    given_second = jnp.concatenate([second_far.astype(BF16), second_near.astype(BF16)])
    given_second, late_first = lax.optimization_barrier((given_second, first))
    second_other = handed(given_second, (0, 1))
    second_query = to_query(late_first, q_weight[0])
    second_keys, second_values = cache(
        jnp.concatenate([second_near, second_far]) + second_other
    )
    second_sum = attend(
        second_query, query_gain[0], second_keys, second_values, live, o_weight[0], gate
    )
    second = added(first, jnp.sum(gathered(second_sum, "tp").astype(F32), axis=0))

    def placed(ours, theirs):
        near = theirs.shape[0] // 2
        turned = jnp.concatenate([theirs[near:], theirs[:near]])
        return jnp.where(section == 0, ours, turned)[None, None, :, None, :]

    keys = placed(first_keys, second_keys)
    values = placed(first_values, second_values)
    section_out = jnp.where(section == 0, first, second)
    return (keys, values, section_out[None])


def solution(mesh):
    devices = mesh.devices
    fine = Mesh(
        devices.reshape(4, 4, 2, devices.shape[1], devices.shape[2]),
        ("far", "row", "core", "section", "tp"),
    )
    return jax.shard_map(
        body,
        mesh=fine,
        in_specs=(
            P(None, None, SEQ),
            P(SEQ, ("section", "tp"), None),
            P(SEQ),
            P("section", SEQ, "tp", None),
            P("section", None),
            P("section", SEQ, "tp"),
            P("section", None),
            P("section", "tp", SEQ),
            P("section"),
        ),
        out_specs=(
            P("section", SEQ, None, "tp", None),
            P("section", SEQ, None, "tp", None),
            P("section", None, None, SEQ),
        ),
        check_vma=False,
    )
```

```python
import math

import jax
import jax.numpy as jnp
from jax import lax
from jax.experimental import pallas as pl
from jax.experimental.pallas import tpu as pltpu
from jax.sharding import Mesh, PartitionSpec as P

TILE_TOK = 128
SEQ = ("far", "row", "core")
CHIP = ("far", "row")
SWAP = [(0, 1), (1, 0)]
BF16 = jnp.bfloat16
F32 = jnp.float32


def norm_per_head(values, gain):
    factor = lax.rsqrt(jnp.mean(values * values, axis=-1, keepdims=True) + 1e-05)
    return values * factor * gain.astype(F32)


def exchange(blocks, axis):
    return lax.all_to_all(blocks, axis, 0, 0, tiled=True)


def gathered(block, axis):
    return exchange(jnp.broadcast_to(block[None], (lax.axis_size(axis),) + block.shape), axis)


def after(value, *earlier):
    return lax.optimization_barrier((value, *earlier))[0]


def dealt(rows, run, order):
    count, width = rows.shape

    def deal(rows_ref, halves_ref):
        for place, pair in enumerate(order):
            to = pl.ds(place * run, run)
            halves_ref[0, :, to] = rows_ref[:, pl.ds(2 * pair * run, run)]
            halves_ref[1, :, to] = rows_ref[:, pl.ds((2 * pair + 1) * run, run)]

    return pl.pallas_call(
        deal,
        out_shape=jax.ShapeDtypeStruct((2, count, width // 2), rows.dtype),
        in_specs=[pl.BlockSpec(memory_space=pltpu.VMEM)],
        out_specs=pl.BlockSpec(memory_space=pltpu.VMEM),
        compiler_params=pltpu.CompilerParams(vmem_limit_bytes=4 * 1024 * 1024),
        cost_estimate=pl.CostEstimate(
            flops=0, bytes_accessed=4 * count * width, transcendentals=0
        ),
        name="deal_halves",
    )(rows)


def to_query(state, weights):
    partial_query = sum(
        jnp.dot(block, weight, preferred_element_type=F32)
        for block, weight in zip(state, weights, strict=True)
    ).astype(BF16)
    chips = lax.axis_size(CHIP)
    pieces = exchange(partial_query.reshape(chips, -1, partial_query.shape[1]), CHIP)
    return jnp.sum(pieces.astype(F32), axis=0)


def attend(query, query_gain, keys, values, live, weights, gate):
    positions = query.shape[0]
    head_size = keys.shape[1]
    query = norm_per_head(query.reshape(-1, head_size), query_gain).astype(BF16)
    scores = jnp.dot(query, keys.T, preferred_element_type=F32) / math.sqrt(head_size)
    shares = jnp.where(live, jnp.exp(scores), 0.0)
    shares = (shares / jnp.sum(shares, axis=-1, keepdims=True)).astype(BF16)
    attended = jnp.dot(shares, values, preferred_element_type=F32).astype(BF16)
    everyone = gathered(attended.reshape(positions, -1), CHIP).reshape(-1, weights[0].shape[0])
    return [
        (gate * jnp.dot(everyone, weight, preferred_element_type=F32)).astype(BF16)
        for weight in weights
    ]


def body(
    hidden, features, tiles, key_value_weight, k_gain, q_weight, query_gain, o_weight, attn_gate
):
    head_size = k_gain.shape[1]
    section = lax.axis_index("section")
    core = lax.axis_index("core")
    tensor_count = lax.axis_size("tp")
    fars, rows, cores = (lax.axis_size(name) for name in SEQ)
    chips = fars * rows
    gate = jnp.tanh(attn_gate[0])

    def by_index(index, first, second):
        return jnp.where(index == 0, first, second)

    def to_other_core(block):
        return lax.ppermute(block, "core", SWAP)

    tokens, width = features.shape[1:]
    run = width // (chips * cores * 2)
    order = [
        (far * rows + row) * cores + each
        for each in range(cores)
        for row in range(rows)
        for far in range(fars)
    ]
    pair = exchange(dealt(features[0], run, order), "section").reshape(2 * tokens, -1)
    gathered_tokens = lax.all_gather(pair, "tp", axis=0, tiled=True)

    parts = after(key_value_weight, pair)[0, :, 0, :].reshape(2, run, -1)
    columns = parts.shape[2]
    kept_weight = by_index(section, parts[0], parts[1])
    got_weight = lax.ppermute(by_index(section, parts[1], parts[0]), "section", SWAP)
    both_parts = by_index(
        section, jnp.stack([kept_weight, got_weight]), jnp.stack([got_weight, kept_weight])
    )

    positions = hidden.shape[1]
    by_parity = after(hidden, pair).reshape(chips, cores, positions, -1)
    own = by_index(core, by_parity[:, 0], by_parity[:, 1]).reshape(chips * positions, -1)
    others = by_index(core, by_parity[:, 1], by_parity[:, 0]).reshape(chips * positions, -1)
    state = [own, to_other_core(others)]
    query_weights = [q_weight[0], to_other_core(after(q_weight, pair)[0])]
    output_weights = [o_weight[0], to_other_core(after(o_weight, pair)[0])]

    by_far = gathered(both_parts, "far")
    first_weight = gathered(gathered(by_far[:, 0], "row"), "core").reshape(-1, columns)
    first_query = to_query([after(state[0], first_weight), state[1]], query_weights)

    def projected(weight):
        return jnp.dot(gathered_tokens, weight, preferred_element_type=F32)

    def handed(partial_sum, direction):
        return lax.ppermute(partial_sum, "section", [direction]).astype(F32)

    def cache(total):
        keys = norm_per_head(total[:, :head_size], k_gain[0]).astype(BF16)
        return keys, total[:, head_size:].astype(BF16)

    slots = jnp.arange(2 * tensor_count * tokens, dtype=jnp.int32)
    place = slots // tokens
    slots = (place % 2 * tensor_count + place // 2) * tokens + slots % tokens
    live = slots[None, :] < tiles[0] * TILE_TOK

    first_partial = projected(first_weight)
    first_keys, first_values = cache(
        first_partial + handed(first_partial.astype(BF16), (1, 0))
    )
    second_weight = lax.all_gather(
        after(by_far[:, 1], gathered_tokens), ("core", "row"), axis=0, tiled=False
    ).reshape(-1, columns)
    first_sum = attend(
        first_query, query_gain[0], first_keys, first_values, live, output_weights, gate
    )
    first_sum = jnp.concatenate(first_sum).reshape(tensor_count, -1, columns)
    summed = jnp.sum(exchange(first_sum, "tp").astype(F32), axis=0).astype(BF16)
    everywhere = gathered(summed, ("section", "tp"))[:tensor_count]
    everywhere = everywhere.reshape(2, chips * positions, -1).astype(F32)
    first = [
        (block.astype(F32) + total).astype(BF16)
        for block, total in zip(state, everywhere, strict=True)
    ]

    second_partial = projected(after(second_weight, summed))
    given, late = lax.optimization_barrier((second_partial.astype(BF16), first[0]))
    second_other = handed(given, (0, 1))
    second_query = to_query([late, first[1]], query_weights)
    second_keys, second_values = cache(second_partial + second_other)
    second_sum = attend(
        second_query, query_gain[0], second_keys, second_values, live, output_weights, gate
    )
    second_sum = by_index(core, jnp.stack(second_sum), jnp.stack(second_sum[::-1]))
    shape = (cores, tensor_count) + second_sum.shape[1:]
    second_sum = jnp.broadcast_to(second_sum[:, None], shape).reshape((-1,) + shape[2:])
    second_sum = exchange(second_sum, ("core", "tp")).reshape(shape)

    returned = to_other_core(after(first[1], second_query))
    first = by_index(core, jnp.stack([first[0], returned]), jnp.stack([returned, first[0]]))
    second = (first.astype(F32) + jnp.sum(second_sum.astype(F32), axis=1)).astype(BF16)
    section_out = by_index(section, first, second).reshape(cores, chips, positions, -1)
    section_out = jnp.transpose(section_out, (1, 0, 2, 3)).reshape((1,) + hidden.shape)

    def placed(ours, theirs):
        chosen = by_index(section, ours, theirs).reshape(tensor_count, 2, tokens, head_size)
        return jnp.transpose(chosen, (1, 0, 2, 3)).reshape(1, 1, -1, 1, head_size)

    return (
        placed(first_keys, second_keys),
        placed(first_values, second_values),
        section_out,
    )


def solution(mesh):
    devices = mesh.devices
    fine = Mesh(
        devices.reshape(4, 4, 2, devices.shape[1], devices.shape[2]),
        ("far", "row", "core", "section", "tp"),
    )
    return jax.shard_map(
        body,
        mesh=fine,
        in_specs=(
            P(None, None, SEQ),
            P(SEQ, ("section", "tp"), None),
            P(SEQ),
            P("section", SEQ, "tp", None),
            P("section", None),
            P("section", SEQ, "tp"),
            P("section", None),
            P("section", "tp", SEQ),
            P("section"),
        ),
        out_specs=(
            P("section", SEQ, None, "tp", None),
            P("section", SEQ, None, "tp", None),
            P("section", None, None, SEQ),
        ),
        check_vma=False,
    )
```

```python
import math

import jax
import jax.numpy as jnp
from jax import lax
from jax.experimental import pallas as pl
from jax.experimental.pallas import tpu as pltpu
from jax.sharding import Mesh, PartitionSpec as P

TILE_TOK = 128
SEQ = ("far", "row", "core")
CHIP = ("far", "row")
SWAP = [(0, 1), (1, 0)]
BF16 = jnp.bfloat16
F32 = jnp.float32


def norm_per_head(values, gain):
    factor = lax.rsqrt(jnp.mean(values * values, axis=-1, keepdims=True) + 1e-05)
    return values * factor * gain.astype(F32)


def exchange(blocks, axis):
    return lax.all_to_all(blocks, axis, 0, 0, tiled=True)


def gathered(block, axis):
    return exchange(jnp.broadcast_to(block[None], (lax.axis_size(axis),) + block.shape), axis)


def after(value, *earlier):
    return lax.optimization_barrier((value, *earlier))[0]


def dealt(rows, run, order):
    count, width = rows.shape

    def deal(rows_ref, halves_ref):
        for place, pair in enumerate(order):
            to = pl.ds(place * run, run)
            halves_ref[0, :, to] = rows_ref[:, pl.ds(2 * pair * run, run)]
            halves_ref[1, :, to] = rows_ref[:, pl.ds((2 * pair + 1) * run, run)]

    return pl.pallas_call(
        deal,
        out_shape=jax.ShapeDtypeStruct((2, count, width // 2), rows.dtype),
        in_specs=[pl.BlockSpec(memory_space=pltpu.VMEM)],
        out_specs=pl.BlockSpec(memory_space=pltpu.VMEM),
        compiler_params=pltpu.CompilerParams(vmem_limit_bytes=4 * 1024 * 1024),
        cost_estimate=pl.CostEstimate(
            flops=0, bytes_accessed=4 * count * width, transcendentals=0
        ),
        name="deal_halves",
    )(rows)


def projected(rows, weight, steps=4):
    count, depth = rows.shape
    columns = weight.shape[1]
    part = depth // steps

    def project(rows_ref, weight_ref, sum_ref, rounded_ref):
        step = pl.program_id(0)
        product = jnp.dot(rows_ref[...], weight_ref[...], preferred_element_type=F32)

        @pl.when(step == 0)
        def _():
            sum_ref[...] = product

        @pl.when(step > 0)
        def _():
            sum_ref[...] += product

        @pl.when(step == steps - 1)
        def _():
            rounded_ref[...] = sum_ref[...].astype(rounded_ref.dtype)

    whole = pl.BlockSpec((count, columns), lambda step: (0, 0))
    return pl.pallas_call(
        project,
        grid=(steps,),
        out_shape=(
            jax.ShapeDtypeStruct((count, columns), F32),
            jax.ShapeDtypeStruct((count, columns), BF16),
        ),
        in_specs=[
            pl.BlockSpec((count, part), lambda step: (0, step)),
            pl.BlockSpec((part, columns), lambda step: (step, 0)),
        ],
        out_specs=(whole, whole),
        compiler_params=pltpu.CompilerParams(
            dimension_semantics=("arbitrary",), vmem_limit_bytes=59 * 1024 * 1024
        ),
        cost_estimate=pl.CostEstimate(
            flops=2 * count * depth * columns,
            bytes_accessed=2 * (count + columns) * depth,
            transcendentals=0,
        ),
        name="project",
    )(rows, weight)


def to_query(state, weight):
    partial_query = jnp.dot(state, weight, preferred_element_type=F32).astype(BF16)
    chips = lax.axis_size(CHIP)
    pieces = exchange(partial_query.reshape(chips, -1, partial_query.shape[1]), CHIP)
    return jnp.sum(pieces.astype(F32), axis=0)


def attend(query, query_gain, keys, values, live, weight, gate):
    positions = query.shape[0]
    head_size = keys.shape[1]
    query = norm_per_head(query.reshape(-1, head_size), query_gain).astype(BF16)
    scores = jnp.dot(query, keys.T, preferred_element_type=F32) / math.sqrt(head_size)
    shares = jnp.where(live, jnp.exp(scores), 0.0)
    shares = (shares / jnp.sum(shares, axis=-1, keepdims=True)).astype(BF16)
    attended = jnp.dot(shares, values, preferred_element_type=F32).astype(BF16)
    everyone = gathered(attended.reshape(positions, -1), CHIP).reshape(-1, weight.shape[0])
    return (gate * jnp.dot(everyone, weight, preferred_element_type=F32)).astype(BF16)


def body(
    hidden, features, tiles, key_value_weight, k_gain, q_weight, query_gain, o_weight, attn_gate
):
    head_size = k_gain.shape[1]
    section = lax.axis_index("section")
    core = lax.axis_index("core")
    tensor_count = lax.axis_size("tp")
    fars, rows, cores = (lax.axis_size(name) for name in SEQ)
    chips = fars * rows
    gate = jnp.tanh(attn_gate[0])

    def by_index(index, first, second):
        return jnp.where(index == 0, first, second)

    def to_other_core(block):
        return lax.ppermute(block, "core", SWAP)

    tokens, width = features.shape[1:]
    run = width // (chips * cores * 2)
    order = [
        (far * rows + row) * cores + each
        for each in range(cores)
        for row in range(rows)
        for far in range(fars)
    ]
    pair = exchange(dealt(features[0], run, order), "section").reshape(2 * tokens, -1)
    parts = key_value_weight[0, :, 0, :].reshape(2, run, -1)
    columns = parts.shape[2]
    kept_weight = by_index(section, parts[0], parts[1])
    got_weight = lax.ppermute(by_index(section, parts[1], parts[0]), "section", SWAP)
    gathered_tokens = lax.all_gather(after(pair, got_weight), "tp", axis=0, tiled=True)
    both_parts = by_index(
        section, jnp.stack([kept_weight, got_weight]), jnp.stack([got_weight, kept_weight])
    )

    positions = hidden.shape[1]
    by_parity = after(hidden, pair).reshape(chips, cores, positions, -1)
    own = by_index(core, by_parity[:, 0], by_parity[:, 1]).reshape(chips * positions, -1)
    others = by_index(core, by_parity[:, 1], by_parity[:, 0]).reshape(chips * positions, -1)
    state = jnp.concatenate([own, to_other_core(others)], axis=1)
    query_weight = jnp.concatenate([q_weight[0], to_other_core(after(q_weight, pair)[0])])
    output_weight = jnp.concatenate(
        [o_weight[0], to_other_core(after(o_weight, pair)[0])], axis=1
    )

    by_far = gathered(both_parts, "far")
    first_weight = gathered(gathered(by_far[:, 0], "row"), "core").reshape(-1, columns)
    state, query_weight, first_weight = lax.optimization_barrier(
        (state, query_weight, first_weight)
    )
    first_query, output_weight = lax.optimization_barrier(
        (to_query(state, query_weight), output_weight)
    )

    def handed(partial_sum, direction):
        return lax.ppermute(partial_sum, "section", [direction]).astype(F32)

    def cache(total):
        keys = norm_per_head(total[:, :head_size], k_gain[0]).astype(BF16)
        return keys, total[:, head_size:].astype(BF16)

    slots = jnp.arange(2 * tensor_count * tokens, dtype=jnp.int32)
    place = slots // tokens
    slots = (place % 2 * tensor_count + place // 2) * tokens + slots % tokens
    live = slots[None, :] < tiles[0] * TILE_TOK

    first_partial, given = projected(gathered_tokens, first_weight)
    first_keys, first_values = cache(first_partial + handed(given, (1, 0)))
    second_weight = lax.all_gather(
        after(by_far[:, 1], gathered_tokens), ("core", "row"), axis=0, tiled=False
    ).reshape(-1, columns)
    first_sum = attend(
        first_query,
        query_gain[0],
        first_keys,
        first_values,
        live,
        output_weight,
        gate,
    )
    first_sum = jnp.concatenate([first_sum[:, :columns], first_sum[:, columns:]])
    first_sum = first_sum.reshape(tensor_count, -1, columns)
    summed = jnp.sum(exchange(first_sum, "tp").astype(F32), axis=0).astype(BF16)
    everywhere = gathered(summed, ("section", "tp"))[:tensor_count]
    everywhere = everywhere.reshape(2, chips * positions, -1).astype(F32)
    everywhere = jnp.concatenate([everywhere[0], everywhere[1]], axis=1)
    first = (state.astype(F32) + everywhere).astype(BF16)

    second_partial, given = projected(gathered_tokens, after(second_weight, summed))
    given, late = lax.optimization_barrier((given, first))
    second_other = handed(given, (0, 1))
    second_query = to_query(late, query_weight)
    second_keys, second_values = cache(second_partial + second_other)
    second_sum = attend(
        second_query, query_gain[0], second_keys, second_values, live, output_weight, gate
    )
    second_sum = by_index(
        core,
        jnp.stack([second_sum[:, :columns], second_sum[:, columns:]]),
        jnp.stack([second_sum[:, columns:], second_sum[:, :columns]]),
    )
    shape = (cores, tensor_count) + second_sum.shape[1:]
    second_sum = jnp.broadcast_to(second_sum[:, None], shape).reshape((-1,) + shape[2:])
    second_sum = exchange(second_sum, ("core", "tp")).reshape(shape)

    ours, others = first[:, :columns], after(first, second_query)[:, columns:]
    returned = to_other_core(others)
    first = by_index(core, jnp.stack([ours, returned]), jnp.stack([returned, ours]))
    second = (first.astype(F32) + jnp.sum(second_sum.astype(F32), axis=1)).astype(BF16)
    section_out = by_index(section, first, second).reshape(cores, chips, positions, -1)
    section_out = jnp.transpose(section_out, (1, 0, 2, 3)).reshape((1,) + hidden.shape)

    def placed(ours, theirs):
        chosen = by_index(section, ours, theirs).reshape(tensor_count, 2, tokens, head_size)
        return jnp.transpose(chosen, (1, 0, 2, 3)).reshape(1, 1, -1, 1, head_size)

    return (
        placed(first_keys, second_keys),
        placed(first_values, second_values),
        section_out,
    )


def solution(mesh):
    devices = mesh.devices
    fine = Mesh(
        devices.reshape(4, 4, 2, devices.shape[1], devices.shape[2]),
        ("far", "row", "core", "section", "tp"),
    )
    return jax.shard_map(
        body,
        mesh=fine,
        in_specs=(
            P(None, None, SEQ),
            P(SEQ, ("section", "tp"), None),
            P(SEQ),
            P("section", SEQ, "tp", None),
            P("section", None),
            P("section", SEQ, "tp"),
            P("section", None),
            P("section", "tp", SEQ),
            P("section"),
        ),
        out_specs=(
            P("section", SEQ, None, "tp", None),
            P("section", SEQ, None, "tp", None),
            P("section", None, None, SEQ),
        ),
        check_vma=False,
    )
```

```python
import math

import jax
import jax.numpy as jnp
from jax import lax
from jax.experimental import pallas as pl
from jax.experimental.pallas import tpu as pltpu
from jax.sharding import Mesh, PartitionSpec as P

TILE_TOK = 128
SEQ = ("far", "row", "core")
CHIP = ("far", "row")
SWAP = [(0, 1), (1, 0)]
BF16 = jnp.bfloat16
F32 = jnp.float32


def norm_per_head(values, gain):
    factor = lax.rsqrt(jnp.mean(values * values, axis=-1, keepdims=True) + 1e-05)
    return values * factor * gain.astype(F32)


def exchange(blocks, axis):
    return lax.all_to_all(blocks, axis, 0, 0, tiled=True)


def gathered(block, axis):
    return exchange(jnp.broadcast_to(block[None], (lax.axis_size(axis),) + block.shape), axis)


def after(value, *earlier):
    return lax.optimization_barrier((value, *earlier))[0]


def dealt(rows, run, order):
    count, width = rows.shape

    def deal(rows_ref, halves_ref):
        for place, pair in enumerate(order):
            to = pl.ds(place * run, run)
            halves_ref[0, :, to] = rows_ref[:, pl.ds(2 * pair * run, run)]
            halves_ref[1, :, to] = rows_ref[:, pl.ds((2 * pair + 1) * run, run)]

    return pl.pallas_call(
        deal,
        out_shape=jax.ShapeDtypeStruct((2, count, width // 2), rows.dtype),
        in_specs=[pl.BlockSpec(memory_space=pltpu.VMEM)],
        out_specs=pl.BlockSpec(memory_space=pltpu.VMEM),
        compiler_params=pltpu.CompilerParams(vmem_limit_bytes=4 * 1024 * 1024),
        cost_estimate=pl.CostEstimate(
            flops=0, bytes_accessed=4 * count * width, transcendentals=0
        ),
        name="deal_halves",
    )(rows)


def projected(rows, weight):
    product = jnp.dot(rows, weight, preferred_element_type=F32)
    return product, product.astype(BF16)


def to_query(state, weight):
    partial_query = jnp.dot(state, weight, preferred_element_type=F32).astype(BF16)
    chips = lax.axis_size(CHIP)
    pieces = exchange(partial_query.reshape(chips, -1, partial_query.shape[1]), CHIP)
    return jnp.sum(pieces.astype(F32), axis=0)


def attend(query, query_gain, keys, values, live, weight, gate):
    positions = query.shape[0]
    head_size = keys.shape[1]
    query = norm_per_head(query.reshape(-1, head_size), query_gain).astype(BF16)
    scores = jnp.dot(query, keys.T, preferred_element_type=F32) / math.sqrt(head_size)
    shares = jnp.where(live, jnp.exp(scores), 0.0)
    shares = (shares / jnp.sum(shares, axis=-1, keepdims=True)).astype(BF16)
    attended = jnp.dot(shares, values, preferred_element_type=F32).astype(BF16)
    everyone = gathered(attended.reshape(positions, -1), CHIP).reshape(-1, weight.shape[0])
    return (gate * jnp.dot(everyone, weight, preferred_element_type=F32)).astype(BF16)


def body(
    hidden, features, tiles, key_value_weight, k_gain, q_weight, query_gain, o_weight, attn_gate
):
    head_size = k_gain.shape[1]
    section = lax.axis_index("section")
    core = lax.axis_index("core")
    tensor_count = lax.axis_size("tp")
    fars, rows, cores = (lax.axis_size(name) for name in SEQ)
    chips = fars * rows
    gate = jnp.tanh(attn_gate[0])

    def by_index(index, first, second):
        return jnp.where(index == 0, first, second)

    def to_other_core(block):
        return lax.ppermute(block, "core", SWAP)

    tokens, width = features.shape[1:]
    run = width // (chips * cores * 2)
    order = [
        (far * rows + row) * cores + each
        for each in range(cores)
        for row in range(rows)
        for far in range(fars)
    ]
    pair = exchange(dealt(features[0], run, order), "section").reshape(2 * tokens, -1)
    parts = key_value_weight[0, :, 0, :].reshape(2, run, -1)
    columns = parts.shape[2]
    kept_weight = by_index(section, parts[0], parts[1])
    got_weight = lax.ppermute(by_index(section, parts[1], parts[0]), "section", SWAP)
    gathered_tokens = lax.all_gather(after(pair, got_weight), "tp", axis=0, tiled=True)
    both_parts = by_index(
        section, jnp.stack([kept_weight, got_weight]), jnp.stack([got_weight, kept_weight])
    )

    positions = hidden.shape[1]
    by_parity = after(hidden, pair).reshape(chips, cores, positions, -1)
    own = by_index(core, by_parity[:, 0], by_parity[:, 1]).reshape(chips * positions, -1)
    others = by_index(core, by_parity[:, 1], by_parity[:, 0]).reshape(chips * positions, -1)
    state = jnp.concatenate([own, to_other_core(others)], axis=1)
    query_weight = jnp.concatenate([q_weight[0], to_other_core(after(q_weight, pair)[0])])
    output_weight = jnp.concatenate(
        [o_weight[0], to_other_core(after(o_weight, pair)[0])], axis=1
    )

    by_far = gathered(both_parts, "far")
    first_weight = gathered(gathered(by_far[:, 0], "row"), "core").reshape(-1, columns)
    state, query_weight, first_weight = lax.optimization_barrier(
        (state, query_weight, first_weight)
    )
    first_query, output_weight, gathered_tokens = lax.optimization_barrier(
        (to_query(state, query_weight), output_weight, gathered_tokens)
    )

    def handed(partial_sum, direction):
        return lax.ppermute(partial_sum, "section", [direction]).astype(F32)

    def cache(total):
        keys = norm_per_head(total[:, :head_size], k_gain[0]).astype(BF16)
        return keys, total[:, head_size:].astype(BF16)

    slots = jnp.arange(2 * tensor_count * tokens, dtype=jnp.int32)
    place = slots // tokens
    slots = (place % 2 * tensor_count + place // 2) * tokens + slots % tokens
    live = slots[None, :] < tiles[0] * TILE_TOK

    first_partial, given = projected(gathered_tokens, first_weight)
    first_keys, first_values = cache(first_partial + handed(given, (1, 0)))
    second_weight = lax.all_gather(
        after(by_far[:, 1], gathered_tokens), ("core", "row"), axis=0, tiled=False
    ).reshape(-1, columns)
    first_sum = attend(
        first_query,
        query_gain[0],
        first_keys,
        first_values,
        live,
        output_weight,
        gate,
    )
    first_sum = jnp.concatenate([first_sum[:, :columns], first_sum[:, columns:]])
    first_sum = first_sum.reshape(tensor_count, -1, columns)
    summed = jnp.sum(exchange(first_sum, "tp").astype(F32), axis=0).astype(BF16)
    everywhere = gathered(summed, ("section", "tp"))[:tensor_count]
    everywhere = everywhere.reshape(2, chips * positions, -1).astype(F32)
    everywhere = jnp.concatenate([everywhere[0], everywhere[1]], axis=1)
    first = (state.astype(F32) + everywhere).astype(BF16)

    second_partial, given = projected(gathered_tokens, after(second_weight, summed))
    given, late = lax.optimization_barrier((given, first))
    second_other = handed(given, (0, 1))
    second_query = to_query(late, query_weight)
    second_keys, second_values = cache(second_partial + second_other)
    second_sum = attend(
        second_query, query_gain[0], second_keys, second_values, live, output_weight, gate
    )
    second_sum = by_index(
        core,
        jnp.stack([second_sum[:, :columns], second_sum[:, columns:]]),
        jnp.stack([second_sum[:, columns:], second_sum[:, :columns]]),
    )
    shape = (cores, tensor_count) + second_sum.shape[1:]
    second_sum = jnp.broadcast_to(second_sum[:, None], shape).reshape((-1,) + shape[2:])
    second_sum = exchange(second_sum, ("core", "tp")).reshape(shape)

    ours, others = first[:, :columns], after(first, second_query)[:, columns:]
    returned = to_other_core(others)
    first = by_index(core, jnp.stack([ours, returned]), jnp.stack([returned, ours]))
    second = (first.astype(F32) + jnp.sum(second_sum.astype(F32), axis=1)).astype(BF16)
    section_out = by_index(section, first, second).reshape(cores, chips, positions, -1)
    section_out = jnp.transpose(section_out, (1, 0, 2, 3)).reshape((1,) + hidden.shape)

    def placed(ours, theirs):
        chosen = by_index(section, ours, theirs).reshape(tensor_count, 2, tokens, head_size)
        return jnp.transpose(chosen, (1, 0, 2, 3)).reshape(1, 1, -1, 1, head_size)

    return (
        placed(first_keys, second_keys),
        placed(first_values, second_values),
        section_out,
    )


def solution(mesh):
    devices = mesh.devices
    fine = Mesh(
        devices.reshape(4, 4, 2, devices.shape[1], devices.shape[2]),
        ("far", "row", "core", "section", "tp"),
    )
    return jax.shard_map(
        body,
        mesh=fine,
        in_specs=(
            P(None, None, SEQ),
            P(SEQ, ("section", "tp"), None),
            P(SEQ),
            P("section", SEQ, "tp", None),
            P("section", None),
            P("section", SEQ, "tp"),
            P("section", None),
            P("section", "tp", SEQ),
            P("section"),
        ),
        out_specs=(
            P("section", SEQ, None, "tp", None),
            P("section", SEQ, None, "tp", None),
            P("section", None, None, SEQ),
        ),
        check_vma=False,
    )
```

```python
import math

import jax
import jax.numpy as jnp
from jax import lax
from jax.experimental import pallas as pl
from jax.experimental.pallas import tpu as pltpu
from jax.sharding import Mesh, PartitionSpec as P

TILE_TOK = 128
SEQ = ("far", "row", "core")
CHIP = ("far", "row")
SWAP = [(0, 1), (1, 0)]
BF16 = jnp.bfloat16
F32 = jnp.float32


def norm_per_head(values, gain):
    factor = lax.rsqrt(jnp.mean(values * values, axis=-1, keepdims=True) + 1e-05)
    return values * factor * gain.astype(F32)


def exchange(blocks, axis):
    return lax.all_to_all(blocks, axis, 0, 0, tiled=True)


def gathered(block, axis):
    return exchange(jnp.broadcast_to(block[None], (lax.axis_size(axis),) + block.shape), axis)


def after(value, *earlier):
    return lax.optimization_barrier((value, *earlier))[0]


def dealt(rows, run, order):
    count, width = rows.shape

    def deal(rows_ref, halves_ref):
        for place, pair in enumerate(order):
            to = pl.ds(place * run, run)
            halves_ref[0, :, to] = rows_ref[:, pl.ds(2 * pair * run, run)]
            halves_ref[1, :, to] = rows_ref[:, pl.ds((2 * pair + 1) * run, run)]

    return pl.pallas_call(
        deal,
        out_shape=jax.ShapeDtypeStruct((2, count, width // 2), rows.dtype),
        in_specs=[pl.BlockSpec(memory_space=pltpu.VMEM)],
        out_specs=pl.BlockSpec(memory_space=pltpu.VMEM),
        compiler_params=pltpu.CompilerParams(vmem_limit_bytes=4 * 1024 * 1024),
        cost_estimate=pl.CostEstimate(
            flops=0, bytes_accessed=4 * count * width, transcendentals=0
        ),
        name="deal_halves",
    )(rows)


def projected(rows, weight):
    product = jnp.dot(rows, weight, preferred_element_type=F32)
    return product, product.astype(BF16)


def to_query(state, weight):
    partial_query = jnp.dot(state, weight, preferred_element_type=F32).astype(BF16)
    chips = lax.axis_size(CHIP)
    pieces = exchange(partial_query.reshape(chips, -1, partial_query.shape[1]), CHIP)
    return jnp.sum(pieces.astype(F32), axis=0)


def attend(query, query_gain, keys, values, live, weight, gate):
    positions = query.shape[0]
    head_size = keys.shape[1]
    query = norm_per_head(query.reshape(-1, head_size), query_gain).astype(BF16)
    scores = jnp.dot(query, keys.T, preferred_element_type=F32) / math.sqrt(head_size)
    shares = jnp.where(live, jnp.exp(scores), 0.0)
    shares = (shares / jnp.sum(shares, axis=-1, keepdims=True)).astype(BF16)
    attended = jnp.dot(shares, values, preferred_element_type=F32).astype(BF16)
    everyone = gathered(attended.reshape(positions, -1), CHIP).reshape(-1, weight.shape[0])
    return (gate * jnp.dot(everyone, weight, preferred_element_type=F32)).astype(BF16)


def body(
    hidden, features, tiles, key_value_weight, k_gain, q_weight, query_gain, o_weight, attn_gate
):
    head_size = k_gain.shape[1]
    section = lax.axis_index("section")
    core = lax.axis_index("core")
    tensor_count = lax.axis_size("tp")
    fars, rows, cores = (lax.axis_size(name) for name in SEQ)
    chips = fars * rows
    gate = jnp.tanh(attn_gate[0])

    def by_index(index, first, second):
        return jnp.where(index == 0, first, second)

    def to_other_core(block):
        return lax.ppermute(block, "core", SWAP)

    tokens, width = features.shape[1:]
    run = width // (chips * cores * 2)
    order = [
        (far * rows + row) * cores + each
        for each in range(cores)
        for row in range(rows)
        for far in range(fars)
    ]
    pair = exchange(dealt(features[0], run, order), "section").reshape(2 * tokens, -1)
    parts = key_value_weight[0, :, 0, :].reshape(2, run, -1)
    columns = parts.shape[2]
    kept_weight = by_index(section, parts[0], parts[1])
    got_weight = lax.ppermute(by_index(section, parts[1], parts[0]), "section", SWAP)
    gathered_tokens = lax.all_gather(after(pair, got_weight), "tp", axis=0, tiled=True)
    both_parts = by_index(
        section, jnp.stack([kept_weight, got_weight]), jnp.stack([got_weight, kept_weight])
    )

    positions = hidden.shape[1]
    by_parity = after(hidden, pair).reshape(chips, cores, positions, -1)
    own = by_index(core, by_parity[:, 0], by_parity[:, 1]).reshape(chips * positions, -1)
    others = by_index(core, by_parity[:, 1], by_parity[:, 0]).reshape(chips * positions, -1)
    state = jnp.concatenate([own, to_other_core(others)], axis=1)
    query_weight = jnp.concatenate([q_weight[0], to_other_core(after(q_weight, pair)[0])])
    output_weight = jnp.concatenate(
        [o_weight[0], to_other_core(after(o_weight, pair)[0])], axis=1
    )

    by_far = gathered(both_parts, "far")
    first_weight = gathered(gathered(by_far[:, 0], "row"), "core").reshape(-1, columns)
    state, query_weight, first_weight = lax.optimization_barrier(
        (state, query_weight, first_weight)
    )
    first_query, output_weight, gathered_tokens = lax.optimization_barrier(
        (to_query(state, query_weight), output_weight, gathered_tokens)
    )

    def handed(partial_sum, direction):
        return lax.ppermute(partial_sum, "section", [direction]).astype(F32)

    def cache(total):
        keys = norm_per_head(total[:, :head_size], k_gain[0]).astype(BF16)
        return keys, total[:, head_size:].astype(BF16)

    slots = jnp.arange(2 * tensor_count * tokens, dtype=jnp.int32)
    place = slots // tokens
    slots = (place % 2 * tensor_count + place // 2) * tokens + slots % tokens
    live = slots[None, :] < tiles[0] * TILE_TOK

    first_partial, given = projected(gathered_tokens, first_weight)
    first_keys, first_values = cache(first_partial + handed(given, (1, 0)))
    second_weight = lax.all_gather(
        after(by_far[:, 1], gathered_tokens), ("core", "row"), axis=0, tiled=False
    ).reshape(-1, columns)
    first_sum = attend(
        first_query,
        query_gain[0],
        first_keys,
        first_values,
        live,
        output_weight,
        gate,
    )
    first_sum, second_weight = lax.optimization_barrier((first_sum, second_weight))
    first_sum = jnp.concatenate([first_sum[:, :columns], first_sum[:, columns:]])
    first_sum = first_sum.reshape(tensor_count, -1, columns)
    summed = jnp.sum(exchange(first_sum, "tp").astype(F32), axis=0).astype(BF16)
    everywhere = gathered(summed, ("section", "tp"))[:tensor_count]
    everywhere = everywhere.reshape(2, chips * positions, -1).astype(F32)
    everywhere = jnp.concatenate([everywhere[0], everywhere[1]], axis=1)
    first = (state.astype(F32) + everywhere).astype(BF16)

    second_partial, given = projected(gathered_tokens, second_weight)
    given, late = lax.optimization_barrier((given, first))
    second_other = handed(given, (0, 1))
    second_query = to_query(late, query_weight)
    second_keys, second_values = cache(second_partial + second_other)
    second_sum = attend(
        second_query, query_gain[0], second_keys, second_values, live, output_weight, gate
    )
    second_sum = by_index(
        core,
        jnp.stack([second_sum[:, :columns], second_sum[:, columns:]]),
        jnp.stack([second_sum[:, columns:], second_sum[:, :columns]]),
    )
    shape = (cores, tensor_count) + second_sum.shape[1:]
    second_sum = jnp.broadcast_to(second_sum[:, None], shape).reshape((-1,) + shape[2:])
    second_sum = exchange(second_sum, ("core", "tp")).reshape(shape)

    ours, others = first[:, :columns], after(first, second_query)[:, columns:]
    returned = to_other_core(others)
    first = by_index(core, jnp.stack([ours, returned]), jnp.stack([returned, ours]))
    second = (first.astype(F32) + jnp.sum(second_sum.astype(F32), axis=1)).astype(BF16)
    section_out = by_index(section, first, second).reshape(cores, chips, positions, -1)
    section_out = jnp.transpose(section_out, (1, 0, 2, 3)).reshape((1,) + hidden.shape)

    def placed(ours, theirs):
        chosen = by_index(section, ours, theirs).reshape(tensor_count, 2, tokens, head_size)
        return jnp.transpose(chosen, (1, 0, 2, 3)).reshape(1, 1, -1, 1, head_size)

    return (
        placed(first_keys, second_keys),
        placed(first_values, second_values),
        section_out,
    )


def solution(mesh):
    devices = mesh.devices
    fine = Mesh(
        devices.reshape(4, 4, 2, devices.shape[1], devices.shape[2]),
        ("far", "row", "core", "section", "tp"),
    )
    return jax.shard_map(
        body,
        mesh=fine,
        in_specs=(
            P(None, None, SEQ),
            P(SEQ, ("section", "tp"), None),
            P(SEQ),
            P("section", SEQ, "tp", None),
            P("section", None),
            P("section", SEQ, "tp"),
            P("section", None),
            P("section", "tp", SEQ),
            P("section"),
        ),
        out_specs=(
            P("section", SEQ, None, "tp", None),
            P("section", SEQ, None, "tp", None),
            P("section", None, None, SEQ),
        ),
        check_vma=False,
    )
```

```python
import math

import jax
import jax.numpy as jnp
from jax import lax
from jax.experimental import pallas as pl
from jax.experimental.pallas import tpu as pltpu
from jax.sharding import Mesh, PartitionSpec as P

TILE_TOK = 128
SEQ = ("far", "row", "core")
CHIP = ("far", "row")
SWAP = [(0, 1), (1, 0)]
BF16 = jnp.bfloat16
F32 = jnp.float32


def norm_per_head(values, gain):
    factor = lax.rsqrt(jnp.mean(values * values, axis=-1, keepdims=True) + 1e-05)
    return values * factor * gain.astype(F32)


def exchange(blocks, axis):
    return lax.all_to_all(blocks, axis, 0, 0, tiled=True)


def gathered(block, axis):
    return exchange(jnp.broadcast_to(block[None], (lax.axis_size(axis),) + block.shape), axis)


def after(value, *earlier):
    return lax.optimization_barrier((value, *earlier))[0]


def dealt(rows, run, order):
    count, width = rows.shape

    def deal(rows_ref, halves_ref):
        for place, pair in enumerate(order):
            to = pl.ds(place * run, run)
            halves_ref[0, :, to] = rows_ref[:, pl.ds(2 * pair * run, run)]
            halves_ref[1, :, to] = rows_ref[:, pl.ds((2 * pair + 1) * run, run)]

    return pl.pallas_call(
        deal,
        out_shape=jax.ShapeDtypeStruct((2, count, width // 2), rows.dtype),
        in_specs=[pl.BlockSpec(memory_space=pltpu.VMEM)],
        out_specs=pl.BlockSpec(memory_space=pltpu.VMEM),
        compiler_params=pltpu.CompilerParams(vmem_limit_bytes=4 * 1024 * 1024),
        cost_estimate=pl.CostEstimate(
            flops=0, bytes_accessed=4 * count * width, transcendentals=0
        ),
        name="deal_halves",
    )(rows)


def turned(parts, place):
    count = len(parts)

    def turn(place_ref, *refs):
        for back, part_ref in enumerate(refs[:-1]):
            refs[-1][lax.rem(place_ref[0] + (count - back), count)] = part_ref[...]

    vmem = pl.BlockSpec(memory_space=pltpu.VMEM)
    return pl.pallas_call(
        turn,
        out_shape=jax.ShapeDtypeStruct((count,) + parts[0].shape, parts[0].dtype),
        in_specs=[pl.BlockSpec(memory_space=pltpu.SMEM)] + [vmem] * count,
        out_specs=vmem,
        compiler_params=pltpu.CompilerParams(vmem_limit_bytes=4 * 1024 * 1024),
        cost_estimate=pl.CostEstimate(
            flops=0, bytes_accessed=4 * count * parts[0].size, transcendentals=0
        ),
        name="turn_parts",
    )(place.reshape(1), *parts)


def projected(rows, weight):
    product = jnp.dot(rows, weight, preferred_element_type=F32)
    return product, product.astype(BF16)


def to_query(state, weight):
    partial_query = jnp.dot(state, weight, preferred_element_type=F32).astype(BF16)
    chips = lax.axis_size(CHIP)
    pieces = exchange(partial_query.reshape(chips, -1, partial_query.shape[1]), CHIP)
    return jnp.sum(pieces.astype(F32), axis=0)


def attend(query, query_gain, keys, values, live, weight, gate):
    positions = query.shape[0]
    head_size = keys.shape[1]
    query = norm_per_head(query.reshape(-1, head_size), query_gain).astype(BF16)
    scores = jnp.dot(query, keys.T, preferred_element_type=F32) / math.sqrt(head_size)
    shares = jnp.where(live, jnp.exp(scores), 0.0)
    shares = (shares / jnp.sum(shares, axis=-1, keepdims=True)).astype(BF16)
    attended = jnp.dot(shares, values, preferred_element_type=F32).astype(BF16)
    everyone = gathered(attended.reshape(positions, -1), CHIP).reshape(-1, weight.shape[0])
    return (gate * jnp.dot(everyone, weight, preferred_element_type=F32)).astype(BF16)


def body(
    hidden, features, tiles, key_value_weight, k_gain, q_weight, query_gain, o_weight, attn_gate
):
    head_size = k_gain.shape[1]
    section = lax.axis_index("section")
    core = lax.axis_index("core")
    tensor_count = lax.axis_size("tp")
    fars, rows, cores = (lax.axis_size(name) for name in SEQ)
    chips = fars * rows
    gate = jnp.tanh(attn_gate[0])

    def by_index(index, first, second):
        return jnp.where(index == 0, first, second)

    def to_other_core(block):
        return lax.ppermute(block, "core", SWAP)

    tokens, width = features.shape[1:]
    run = width // (chips * cores * 2)
    order = [
        (far * rows + row) * cores + each
        for each in range(cores)
        for row in range(rows)
        for far in range(fars)
    ]
    pair = exchange(dealt(features[0], run, order), "section").reshape(2 * tokens, -1)
    parts = key_value_weight[0, :, 0, :].reshape(2, run, -1)
    columns = parts.shape[2]
    kept_weight = by_index(section, parts[0], parts[1])
    got_weight = lax.ppermute(by_index(section, parts[1], parts[0]), "section", SWAP)
    gathered_tokens = lax.all_gather(after(pair, got_weight), "tp", axis=0, tiled=True)
    first_part = by_index(section, kept_weight, got_weight)
    second_part = by_index(section, got_weight, kept_weight)

    positions = hidden.shape[1]
    by_parity = after(hidden, pair).reshape(chips, cores, positions, -1)
    own = by_index(core, by_parity[:, 0], by_parity[:, 1]).reshape(chips * positions, -1)
    others = by_index(core, by_parity[:, 1], by_parity[:, 0]).reshape(chips * positions, -1)
    state = jnp.concatenate([own, to_other_core(others)], axis=1)
    query_weight = jnp.concatenate([q_weight[0], to_other_core(after(q_weight, pair)[0])])
    output_weight = jnp.concatenate(
        [o_weight[0], to_other_core(after(o_weight, pair)[0])], axis=1
    )

    by_far = gathered(first_part, "far")
    first_weight = gathered(gathered(by_far, "row"), "core").reshape(-1, columns)
    early_part = after(second_part, by_far)
    second_parts = [second_part] + [
        lax.ppermute(early_part, "far", [(far, (far + step) % fars) for far in range(fars)])
        for step in range(1, fars)
    ]
    state, query_weight, first_weight, second_parts = lax.optimization_barrier(
        (state, query_weight, first_weight, second_parts)
    )
    second_by_far = turned(second_parts, lax.axis_index("far").astype(jnp.int32))
    first_query, output_weight, gathered_tokens = lax.optimization_barrier(
        (to_query(state, query_weight), output_weight, gathered_tokens)
    )

    def handed(partial_sum, direction):
        return lax.ppermute(partial_sum, "section", [direction]).astype(F32)

    def cache(total):
        keys = norm_per_head(total[:, :head_size], k_gain[0]).astype(BF16)
        return keys, total[:, head_size:].astype(BF16)

    slots = jnp.arange(2 * tensor_count * tokens, dtype=jnp.int32)
    place = slots // tokens
    slots = (place % 2 * tensor_count + place // 2) * tokens + slots % tokens
    live = slots[None, :] < tiles[0] * TILE_TOK

    first_partial, given = projected(gathered_tokens, first_weight)
    first_keys, first_values = cache(first_partial + handed(given, (1, 0)))
    second_weight = lax.all_gather(
        after(second_by_far, gathered_tokens), ("core", "row"), axis=0, tiled=False
    ).reshape(-1, columns)
    first_sum = attend(
        first_query,
        query_gain[0],
        first_keys,
        first_values,
        live,
        output_weight,
        gate,
    )
    first_sum, second_weight = lax.optimization_barrier((first_sum, second_weight))
    first_sum = jnp.concatenate([first_sum[:, :columns], first_sum[:, columns:]])
    first_sum = first_sum.reshape(tensor_count, -1, columns)
    summed = jnp.sum(exchange(first_sum, "tp").astype(F32), axis=0).astype(BF16)
    everywhere = gathered(summed, ("section", "tp"))[:tensor_count]
    everywhere = everywhere.reshape(2, chips * positions, -1).astype(F32)
    everywhere = jnp.concatenate([everywhere[0], everywhere[1]], axis=1)
    first = (state.astype(F32) + everywhere).astype(BF16)

    second_partial, given = projected(gathered_tokens, second_weight)
    given, late = lax.optimization_barrier((given, first))
    second_other = handed(given, (0, 1))
    second_query = to_query(late, query_weight)
    second_keys, second_values = cache(second_partial + second_other)
    second_sum = attend(
        second_query, query_gain[0], second_keys, second_values, live, output_weight, gate
    )
    second_sum = by_index(
        core,
        jnp.stack([second_sum[:, :columns], second_sum[:, columns:]]),
        jnp.stack([second_sum[:, columns:], second_sum[:, :columns]]),
    )
    shape = (cores, tensor_count) + second_sum.shape[1:]
    second_sum = jnp.broadcast_to(second_sum[:, None], shape).reshape((-1,) + shape[2:])
    second_sum = exchange(second_sum, ("core", "tp")).reshape(shape)

    ours, others = first[:, :columns], after(first, second_query)[:, columns:]
    returned = to_other_core(others)
    first = by_index(core, jnp.stack([ours, returned]), jnp.stack([returned, ours]))
    second = (first.astype(F32) + jnp.sum(second_sum.astype(F32), axis=1)).astype(BF16)
    section_out = by_index(section, first, second).reshape(cores, chips, positions, -1)
    section_out = jnp.transpose(section_out, (1, 0, 2, 3)).reshape((1,) + hidden.shape)

    def placed(ours, theirs):
        chosen = by_index(section, ours, theirs).reshape(tensor_count, 2, tokens, head_size)
        return jnp.transpose(chosen, (1, 0, 2, 3)).reshape(1, 1, -1, 1, head_size)

    return (
        placed(first_keys, second_keys),
        placed(first_values, second_values),
        section_out,
    )


def solution(mesh):
    devices = mesh.devices
    fine = Mesh(
        devices.reshape(4, 4, 2, devices.shape[1], devices.shape[2]),
        ("far", "row", "core", "section", "tp"),
    )
    return jax.shard_map(
        body,
        mesh=fine,
        in_specs=(
            P(None, None, SEQ),
            P(SEQ, ("section", "tp"), None),
            P(SEQ),
            P("section", SEQ, "tp", None),
            P("section", None),
            P("section", SEQ, "tp"),
            P("section", None),
            P("section", "tp", SEQ),
            P("section"),
        ),
        out_specs=(
            P("section", SEQ, None, "tp", None),
            P("section", SEQ, None, "tp", None),
            P("section", None, None, SEQ),
        ),
        check_vma=False,
    )
```

```python
import math

import jax
import jax.numpy as jnp
from jax import lax
from jax.experimental import pallas as pl
from jax.experimental.pallas import tpu as pltpu
from jax.sharding import Mesh, PartitionSpec as P

TILE_TOK = 128
SEQ = ("far", "row", "core")
CHIP = ("far", "row")
SWAP = [(0, 1), (1, 0)]
BF16 = jnp.bfloat16
F32 = jnp.float32


def norm_per_head(values, gain):
    factor = lax.rsqrt(jnp.mean(values * values, axis=-1, keepdims=True) + 1e-05)
    return values * factor * gain.astype(F32)


def exchange(blocks, axis):
    return lax.all_to_all(blocks, axis, 0, 0, tiled=True)


def gathered(block, axis):
    return exchange(jnp.broadcast_to(block[None], (lax.axis_size(axis),) + block.shape), axis)


def after(value, *earlier):
    return lax.optimization_barrier((value, *earlier))[0]


def dealt(rows, run, order):
    count, width = rows.shape

    def deal(rows_ref, halves_ref):
        for place, pair in enumerate(order):
            to = pl.ds(place * run, run)
            halves_ref[0, :, to] = rows_ref[:, pl.ds(2 * pair * run, run)]
            halves_ref[1, :, to] = rows_ref[:, pl.ds((2 * pair + 1) * run, run)]

    return pl.pallas_call(
        deal,
        out_shape=jax.ShapeDtypeStruct((2, count, width // 2), rows.dtype),
        in_specs=[pl.BlockSpec(memory_space=pltpu.VMEM)],
        out_specs=pl.BlockSpec(memory_space=pltpu.VMEM),
        compiler_params=pltpu.CompilerParams(vmem_limit_bytes=4 * 1024 * 1024),
        cost_estimate=pl.CostEstimate(
            flops=0, bytes_accessed=4 * count * width, transcendentals=0
        ),
        name="deal_halves",
    )(rows)


def turned(parts, place):
    count = len(parts)

    def turn(place_ref, *refs):
        for back, part_ref in enumerate(refs[:-1]):
            refs[-1][lax.rem(place_ref[0] + (count - back), count)] = part_ref[...]

    vmem = pl.BlockSpec(memory_space=pltpu.VMEM)
    return pl.pallas_call(
        turn,
        out_shape=jax.ShapeDtypeStruct((count,) + parts[0].shape, parts[0].dtype),
        in_specs=[pl.BlockSpec(memory_space=pltpu.SMEM)] + [vmem] * count,
        out_specs=vmem,
        compiler_params=pltpu.CompilerParams(vmem_limit_bytes=4 * 1024 * 1024),
        cost_estimate=pl.CostEstimate(
            flops=0, bytes_accessed=4 * count * parts[0].size, transcendentals=0
        ),
        name="turn_parts",
    )(place.reshape(1), *parts)


def projected(rows, weight):
    product = jnp.dot(rows, weight, preferred_element_type=F32)
    return product, product.astype(BF16)


def to_query(state, weight):
    partial_query = jnp.dot(state, weight, preferred_element_type=F32).astype(BF16)
    chips = lax.axis_size(CHIP)
    pieces = exchange(partial_query.reshape(chips, -1, partial_query.shape[1]), CHIP)
    return jnp.sum(pieces.astype(F32), axis=0)


def attend(query, query_gain, keys, values, live, weight, gate):
    positions = query.shape[0]
    head_size = keys.shape[1]
    query = norm_per_head(query.reshape(-1, head_size), query_gain).astype(BF16)
    scores = jnp.dot(query, keys.T, preferred_element_type=F32) / math.sqrt(head_size)
    shares = jnp.where(live, jnp.exp(scores), 0.0)
    shares = (shares / jnp.sum(shares, axis=-1, keepdims=True)).astype(BF16)
    attended = jnp.dot(shares, values, preferred_element_type=F32).astype(BF16)
    everyone = gathered(attended.reshape(positions, -1), CHIP).reshape(-1, weight.shape[0])
    return (gate * jnp.dot(everyone, weight, preferred_element_type=F32)).astype(BF16)


def body(
    hidden, features, tiles, key_value_weight, k_gain, q_weight, query_gain, o_weight, attn_gate
):
    head_size = k_gain.shape[1]
    section = lax.axis_index("section")
    core = lax.axis_index("core")
    tensor_count = lax.axis_size("tp")
    fars, rows, cores = (lax.axis_size(name) for name in SEQ)
    chips = fars * rows
    gate = jnp.tanh(attn_gate[0])

    def by_index(index, first, second):
        return jnp.where(index == 0, first, second)

    def to_other_core(block):
        return lax.ppermute(block, "core", SWAP)

    tokens, width = features.shape[1:]
    run = width // (chips * cores * 2)
    order = [
        (far * rows + row) * cores + each
        for each in range(cores)
        for row in range(rows)
        for far in range(fars)
    ]
    pair = exchange(dealt(features[0], run, order), "section").reshape(2 * tokens, -1)
    parts = key_value_weight[0, :, 0, :].reshape(2, run, -1)
    columns = parts.shape[2]
    kept_weight = by_index(section, parts[0], parts[1])
    got_weight = lax.ppermute(by_index(section, parts[1], parts[0]), "section", SWAP)
    gathered_tokens = lax.all_gather(after(pair, got_weight), "tp", axis=0, tiled=True)
    first_part = by_index(section, kept_weight, got_weight)
    second_part = by_index(section, got_weight, kept_weight)

    positions = hidden.shape[1]
    by_parity = after(hidden, pair).reshape(chips, cores, positions, -1)
    own = by_index(core, by_parity[:, 0], by_parity[:, 1]).reshape(chips * positions, -1)
    others = by_index(core, by_parity[:, 1], by_parity[:, 0]).reshape(chips * positions, -1)
    state = jnp.concatenate([own, to_other_core(others)], axis=1)
    query_weight = jnp.concatenate([q_weight[0], to_other_core(after(q_weight, pair)[0])])
    output_weight = jnp.concatenate(
        [o_weight[0], to_other_core(after(o_weight, pair)[0])], axis=1
    )

    by_far = gathered(first_part, "far")
    first_weight = gathered(gathered(by_far, "row"), "core").reshape(-1, columns)
    early_part = after(second_part, first_weight)
    second_parts = [second_part] + [
        lax.ppermute(early_part, "far", [(far, (far + step) % fars) for far in range(fars)])
        for step in range(1, fars)
    ]
    state, query_weight, first_weight = lax.optimization_barrier(
        (state, query_weight, first_weight)
    )
    second_by_far = turned(second_parts, lax.axis_index("far").astype(jnp.int32))
    first_query, output_weight, gathered_tokens = lax.optimization_barrier(
        (to_query(state, query_weight), output_weight, gathered_tokens)
    )

    def handed(partial_sum, direction):
        return lax.ppermute(partial_sum, "section", [direction]).astype(F32)

    def cache(total):
        keys = norm_per_head(total[:, :head_size], k_gain[0]).astype(BF16)
        return keys, total[:, head_size:].astype(BF16)

    slots = jnp.arange(2 * tensor_count * tokens, dtype=jnp.int32)
    place = slots // tokens
    slots = (place % 2 * tensor_count + place // 2) * tokens + slots % tokens
    live = slots[None, :] < tiles[0] * TILE_TOK

    first_partial, given = projected(gathered_tokens, first_weight)
    first_keys, first_values = cache(first_partial + handed(given, (1, 0)))
    second_weight = lax.all_gather(
        after(second_by_far, gathered_tokens), ("core", "row"), axis=0, tiled=False
    ).reshape(-1, columns)
    first_sum = attend(
        first_query,
        query_gain[0],
        first_keys,
        first_values,
        live,
        output_weight,
        gate,
    )
    first_sum = jnp.concatenate([first_sum[:, :columns], first_sum[:, columns:]])
    first_sum = first_sum.reshape(tensor_count, -1, columns)
    summed = jnp.sum(exchange(first_sum, "tp").astype(F32), axis=0).astype(BF16)
    summed, second_weight = lax.optimization_barrier((summed, second_weight))
    everywhere = gathered(summed, ("section", "tp"))[:tensor_count]
    everywhere = everywhere.reshape(2, chips * positions, -1).astype(F32)
    everywhere = jnp.concatenate([everywhere[0], everywhere[1]], axis=1)
    first = (state.astype(F32) + everywhere).astype(BF16)

    second_partial, given = projected(gathered_tokens, second_weight)
    given, late = lax.optimization_barrier((given, first))
    second_other = handed(given, (0, 1))
    second_query = to_query(late, query_weight)
    second_keys, second_values = cache(second_partial + second_other)
    second_sum = attend(
        second_query, query_gain[0], second_keys, second_values, live, output_weight, gate
    )
    second_sum = by_index(
        core,
        jnp.stack([second_sum[:, :columns], second_sum[:, columns:]]),
        jnp.stack([second_sum[:, columns:], second_sum[:, :columns]]),
    )
    shape = (cores, tensor_count) + second_sum.shape[1:]
    second_sum = jnp.broadcast_to(second_sum[:, None], shape).reshape((-1,) + shape[2:])
    second_sum = exchange(second_sum, ("core", "tp")).reshape(shape)

    ours, others = first[:, :columns], after(first, second_query)[:, columns:]
    returned = to_other_core(others)
    first = by_index(core, jnp.stack([ours, returned]), jnp.stack([returned, ours]))
    second = (first.astype(F32) + jnp.sum(second_sum.astype(F32), axis=1)).astype(BF16)
    section_out = by_index(section, first, second).reshape(cores, chips, positions, -1)
    section_out = jnp.transpose(section_out, (1, 0, 2, 3)).reshape((1,) + hidden.shape)

    def placed(ours, theirs):
        chosen = by_index(section, ours, theirs).reshape(tensor_count, 2, tokens, head_size)
        return jnp.transpose(chosen, (1, 0, 2, 3)).reshape(1, 1, -1, 1, head_size)

    return (
        placed(first_keys, second_keys),
        placed(first_values, second_values),
        section_out,
    )


def solution(mesh):
    devices = mesh.devices
    fine = Mesh(
        devices.reshape(4, 4, 2, devices.shape[1], devices.shape[2]),
        ("far", "row", "core", "section", "tp"),
    )
    return jax.shard_map(
        body,
        mesh=fine,
        in_specs=(
            P(None, None, SEQ),
            P(SEQ, ("section", "tp"), None),
            P(SEQ),
            P("section", SEQ, "tp", None),
            P("section", None),
            P("section", SEQ, "tp"),
            P("section", None),
            P("section", "tp", SEQ),
            P("section"),
        ),
        out_specs=(
            P("section", SEQ, None, "tp", None),
            P("section", SEQ, None, "tp", None),
            P("section", None, None, SEQ),
        ),
        check_vma=False,
    )
```

```python
import math

import jax
import jax.numpy as jnp
from jax import lax
from jax.experimental import pallas as pl
from jax.experimental.pallas import tpu as pltpu
from jax.sharding import Mesh, PartitionSpec as P

TILE_TOK = 128
SEQ = ("far", "row", "core")
CHIP = ("far", "row")
SWAP = [(0, 1), (1, 0)]
BF16 = jnp.bfloat16
F32 = jnp.float32


def norm_per_head(values, gain):
    factor = lax.rsqrt(jnp.mean(values * values, axis=-1, keepdims=True) + 1e-05)
    return values * factor * gain.astype(F32)


def exchange(blocks, axis):
    return lax.all_to_all(blocks, axis, 0, 0, tiled=True)


def gathered(block, axis):
    return exchange(jnp.broadcast_to(block[None], (lax.axis_size(axis),) + block.shape), axis)


def after(value, *earlier):
    return lax.optimization_barrier((value, *earlier))[0]


def dealt(rows, run, order):
    count, width = rows.shape

    def deal(rows_ref, halves_ref):
        for place, pair in enumerate(order):
            to = pl.ds(place * run, run)
            halves_ref[0, :, to] = rows_ref[:, pl.ds(2 * pair * run, run)]
            halves_ref[1, :, to] = rows_ref[:, pl.ds((2 * pair + 1) * run, run)]

    return pl.pallas_call(
        deal,
        out_shape=jax.ShapeDtypeStruct((2, count, width // 2), rows.dtype),
        in_specs=[pl.BlockSpec(memory_space=pltpu.VMEM)],
        out_specs=pl.BlockSpec(memory_space=pltpu.VMEM),
        compiler_params=pltpu.CompilerParams(vmem_limit_bytes=4 * 1024 * 1024),
        cost_estimate=pl.CostEstimate(
            flops=0, bytes_accessed=4 * count * width, transcendentals=0
        ),
        name="deal_halves",
    )(rows)


def projected(rows, weight):
    product = jnp.dot(rows, weight, preferred_element_type=F32)
    return product, product.astype(BF16)


def to_query(state, weight):
    partial_query = jnp.dot(state, weight, preferred_element_type=F32).astype(BF16)
    chips = lax.axis_size(CHIP)
    pieces = exchange(partial_query.reshape(chips, -1, partial_query.shape[1]), CHIP)
    return jnp.sum(pieces.astype(F32), axis=0)


def attend(query, query_gain, keys, values, live, weight, gate):
    positions = query.shape[0]
    head_size = keys.shape[1]
    query = norm_per_head(query.reshape(-1, head_size), query_gain).astype(BF16)
    scores = jnp.dot(query, keys.T, preferred_element_type=F32) / math.sqrt(head_size)
    shares = jnp.where(live, jnp.exp(scores), 0.0)
    shares = (shares / jnp.sum(shares, axis=-1, keepdims=True)).astype(BF16)
    attended = jnp.dot(shares, values, preferred_element_type=F32).astype(BF16)
    everyone = gathered(attended.reshape(positions, -1), CHIP).reshape(-1, weight.shape[0])
    return (gate * jnp.dot(everyone, weight, preferred_element_type=F32)).astype(BF16)


def body(
    hidden, features, tiles, key_value_weight, k_gain, q_weight, query_gain, o_weight, attn_gate
):
    head_size = k_gain.shape[1]
    section = lax.axis_index("section")
    core = lax.axis_index("core")
    tensor_count = lax.axis_size("tp")
    fars, rows, cores = (lax.axis_size(name) for name in SEQ)
    chips = fars * rows
    gate = jnp.tanh(attn_gate[0])

    def by_index(index, first, second):
        return jnp.where(index == 0, first, second)

    def to_other_core(block):
        return lax.ppermute(block, "core", SWAP)

    tokens, width = features.shape[1:]
    run = width // (chips * cores * 2)
    order = [
        (far * rows + row) * cores + each
        for each in range(cores)
        for row in range(rows)
        for far in range(fars)
    ]
    pair = exchange(dealt(features[0], run, order), "section").reshape(2 * tokens, -1)
    parts = key_value_weight[0, :, 0, :].reshape(2, run, -1)
    columns = parts.shape[2]
    kept_weight = by_index(section, parts[0], parts[1])
    got_weight = lax.ppermute(by_index(section, parts[1], parts[0]), "section", SWAP)
    gathered_tokens = lax.all_gather(after(pair, got_weight), "tp", axis=0, tiled=True)
    both_parts = by_index(
        section, jnp.stack([kept_weight, got_weight]), jnp.stack([got_weight, kept_weight])
    )

    positions = hidden.shape[1]
    by_parity = after(hidden, pair).reshape(chips, cores, positions, -1)
    own = by_index(core, by_parity[:, 0], by_parity[:, 1]).reshape(chips * positions, -1)
    others = by_index(core, by_parity[:, 1], by_parity[:, 0]).reshape(chips * positions, -1)
    state = jnp.concatenate([own, to_other_core(others)], axis=1)
    query_weight = jnp.concatenate([q_weight[0], to_other_core(after(q_weight, pair)[0])])
    output_weight = jnp.concatenate(
        [o_weight[0], to_other_core(after(o_weight, pair)[0])], axis=1
    )

    by_far = gathered(both_parts, "far")
    first_weight = gathered(gathered(by_far[:, 0], "row"), "core").reshape(-1, columns)
    state, query_weight, first_weight = lax.optimization_barrier(
        (state, query_weight, first_weight)
    )
    first_query, output_weight, gathered_tokens = lax.optimization_barrier(
        (to_query(state, query_weight), output_weight, gathered_tokens)
    )

    def handed(partial_sum, direction):
        return lax.ppermute(partial_sum, "section", [direction]).astype(F32)

    def cache(total):
        keys = norm_per_head(total[:, :head_size], k_gain[0]).astype(BF16)
        return keys, total[:, head_size:].astype(BF16)

    slots = jnp.arange(2 * tensor_count * tokens, dtype=jnp.int32)
    place = slots // tokens
    slots = (place % 2 * tensor_count + place // 2) * tokens + slots % tokens
    live = slots[None, :] < tiles[0] * TILE_TOK

    first_partial, given = projected(gathered_tokens, first_weight)
    first_keys, first_values = cache(first_partial + handed(given, (1, 0)))
    second_weight = lax.all_gather(
        after(by_far[:, 1], gathered_tokens), ("core", "row"), axis=0, tiled=False
    ).reshape(-1, columns)
    first_sum = attend(
        first_query,
        query_gain[0],
        first_keys,
        first_values,
        live,
        output_weight,
        gate,
    )
    first_sum, second_weight = lax.optimization_barrier((first_sum, second_weight))
    first_sum = jnp.concatenate([first_sum[:, :columns], first_sum[:, columns:]])
    everywhere = gathered(first_sum, ("section", "tp"))[:tensor_count]
    everywhere = jnp.sum(everywhere.astype(F32), axis=0)
    everywhere = everywhere.reshape(2, chips * positions, -1)
    everywhere = jnp.concatenate([everywhere[0], everywhere[1]], axis=1)
    first = (state.astype(F32) + everywhere).astype(BF16)

    second_partial, given = projected(gathered_tokens, second_weight)
    given, late = lax.optimization_barrier((given, first))
    second_other = handed(given, (0, 1))
    second_query = to_query(late, query_weight)
    second_keys, second_values = cache(second_partial + second_other)
    second_sum = attend(
        second_query, query_gain[0], second_keys, second_values, live, output_weight, gate
    )
    second_sum = by_index(
        core,
        jnp.stack([second_sum[:, :columns], second_sum[:, columns:]]),
        jnp.stack([second_sum[:, columns:], second_sum[:, :columns]]),
    )
    shape = (cores, tensor_count) + second_sum.shape[1:]
    second_sum = jnp.broadcast_to(second_sum[:, None], shape).reshape((-1,) + shape[2:])
    second_sum = exchange(second_sum, ("core", "tp")).reshape(shape)

    ours, others = first[:, :columns], after(first, second_query)[:, columns:]
    returned = to_other_core(others)
    first = by_index(core, jnp.stack([ours, returned]), jnp.stack([returned, ours]))
    second = (first.astype(F32) + jnp.sum(second_sum.astype(F32), axis=1)).astype(BF16)
    section_out = by_index(section, first, second).reshape(cores, chips, positions, -1)
    section_out = jnp.transpose(section_out, (1, 0, 2, 3)).reshape((1,) + hidden.shape)

    def placed(ours, theirs):
        chosen = by_index(section, ours, theirs).reshape(tensor_count, 2, tokens, head_size)
        return jnp.transpose(chosen, (1, 0, 2, 3)).reshape(1, 1, -1, 1, head_size)

    return (
        placed(first_keys, second_keys),
        placed(first_values, second_values),
        section_out,
    )


def solution(mesh):
    devices = mesh.devices
    fine = Mesh(
        devices.reshape(4, 4, 2, devices.shape[1], devices.shape[2]),
        ("far", "row", "core", "section", "tp"),
    )
    return jax.shard_map(
        body,
        mesh=fine,
        in_specs=(
            P(None, None, SEQ),
            P(SEQ, ("section", "tp"), None),
            P(SEQ),
            P("section", SEQ, "tp", None),
            P("section", None),
            P("section", SEQ, "tp"),
            P("section", None),
            P("section", "tp", SEQ),
            P("section"),
        ),
        out_specs=(
            P("section", SEQ, None, "tp", None),
            P("section", SEQ, None, "tp", None),
            P("section", None, None, SEQ),
        ),
        check_vma=False,
    )
```

```python
import math

import jax
import jax.numpy as jnp
from jax import lax
from jax.experimental import pallas as pl
from jax.experimental.pallas import tpu as pltpu
from jax.sharding import Mesh, PartitionSpec as P

TILE_TOK = 128
SEQ = ("far", "row", "core")
CHIP = ("far", "row")
SWAP = [(0, 1), (1, 0)]
BF16 = jnp.bfloat16
F32 = jnp.float32


def norm_per_head(values, gain):
    factor = lax.rsqrt(jnp.mean(values * values, axis=-1, keepdims=True) + 1e-05)
    return values * factor * gain.astype(F32)


def exchange(blocks, axis):
    return lax.all_to_all(blocks, axis, 0, 0, tiled=True)


def gathered(block, axis):
    return exchange(jnp.broadcast_to(block[None], (lax.axis_size(axis),) + block.shape), axis)


def after(value, *earlier):
    return lax.optimization_barrier((value, *earlier))[0]


def dealt(rows, run, order):
    count, width = rows.shape

    def deal(rows_ref, halves_ref):
        for place, pair in enumerate(order):
            to = pl.ds(place * run, run)
            halves_ref[0, :, to] = rows_ref[:, pl.ds(2 * pair * run, run)]
            halves_ref[1, :, to] = rows_ref[:, pl.ds((2 * pair + 1) * run, run)]

    return pl.pallas_call(
        deal,
        out_shape=jax.ShapeDtypeStruct((2, count, width // 2), rows.dtype),
        in_specs=[pl.BlockSpec(memory_space=pltpu.VMEM)],
        out_specs=pl.BlockSpec(memory_space=pltpu.VMEM),
        compiler_params=pltpu.CompilerParams(vmem_limit_bytes=4 * 1024 * 1024),
        cost_estimate=pl.CostEstimate(
            flops=0, bytes_accessed=4 * count * width, transcendentals=0
        ),
        name="deal_halves",
    )(rows)


def projected(rows, weight):
    product = jnp.dot(rows, weight, preferred_element_type=F32)
    return product, product.astype(BF16)


def to_query(state, weight):
    partial_query = jnp.dot(state, weight, preferred_element_type=F32).astype(BF16)
    chips = lax.axis_size(CHIP)
    pieces = exchange(partial_query.reshape(chips, -1, partial_query.shape[1]), CHIP)
    return jnp.sum(pieces.astype(F32), axis=0)


def attend(query, query_gain, keys, values, live, weight, gate):
    positions = query.shape[0]
    head_size = keys.shape[1]
    query = norm_per_head(query.reshape(-1, head_size), query_gain).astype(BF16)
    scores = jnp.dot(query, keys.T, preferred_element_type=F32) / math.sqrt(head_size)
    shares = jnp.where(live, jnp.exp(scores), 0.0)
    shares = (shares / jnp.sum(shares, axis=-1, keepdims=True)).astype(BF16)
    attended = jnp.dot(shares, values, preferred_element_type=F32).astype(BF16)
    everyone = gathered(attended.reshape(positions, -1), CHIP).reshape(-1, weight.shape[0])
    return (gate * jnp.dot(everyone, weight, preferred_element_type=F32)).astype(BF16)


def body(
    hidden, features, tiles, key_value_weight, k_gain, q_weight, query_gain, o_weight, attn_gate
):
    head_size = k_gain.shape[1]
    section = lax.axis_index("section")
    core = lax.axis_index("core")
    tensor_count = lax.axis_size("tp")
    fars, rows, cores = (lax.axis_size(name) for name in SEQ)
    chips = fars * rows
    gate = jnp.tanh(attn_gate[0])

    def by_index(index, first, second):
        return jnp.where(index == 0, first, second)

    def to_other_core(block):
        return lax.ppermute(block, "core", SWAP)

    tokens, width = features.shape[1:]
    run = width // (chips * cores * 2)
    order = [
        (far * rows + row) * cores + each
        for each in range(cores)
        for row in range(rows)
        for far in range(fars)
    ]
    pair = exchange(dealt(features[0], run, order), "section").reshape(2 * tokens, -1)
    parts = key_value_weight[0, :, 0, :].reshape(2, run, -1)
    columns = parts.shape[2]
    kept_weight = by_index(section, parts[0], parts[1])
    got_weight = lax.ppermute(by_index(section, parts[1], parts[0]), "section", SWAP)
    gathered_tokens = lax.all_gather(after(pair, got_weight), "tp", axis=0, tiled=True)
    both_parts = by_index(
        section, jnp.stack([kept_weight, got_weight]), jnp.stack([got_weight, kept_weight])
    )

    positions = hidden.shape[1]
    by_parity = after(hidden, pair).reshape(chips, cores, positions, -1)
    own = by_index(core, by_parity[:, 0], by_parity[:, 1]).reshape(chips * positions, -1)
    others = by_index(core, by_parity[:, 1], by_parity[:, 0]).reshape(chips * positions, -1)
    state = jnp.concatenate([own, to_other_core(others)], axis=1)
    query_weight = jnp.concatenate([q_weight[0], to_other_core(after(q_weight, pair)[0])])
    output_weight = jnp.concatenate(
        [o_weight[0], to_other_core(after(o_weight, pair)[0])], axis=1
    )

    by_far = gathered(both_parts, "far")
    first_weight = gathered(gathered(by_far[:, 0], "row"), "core").reshape(-1, columns)
    state, query_weight, first_weight = lax.optimization_barrier(
        (state, query_weight, first_weight)
    )
    first_query, output_weight, gathered_tokens = lax.optimization_barrier(
        (to_query(state, query_weight), output_weight, gathered_tokens)
    )

    def handed(partial_sum, direction):
        return lax.ppermute(partial_sum, "section", [direction]).astype(F32)

    def cache(total):
        keys = norm_per_head(total[:, :head_size], k_gain[0]).astype(BF16)
        return keys, total[:, head_size:].astype(BF16)

    slots = jnp.arange(2 * tensor_count * tokens, dtype=jnp.int32)
    place = slots // tokens
    slots = (place % 2 * tensor_count + place // 2) * tokens + slots % tokens
    live = slots[None, :] < tiles[0] * TILE_TOK

    first_partial, given = projected(gathered_tokens, first_weight)
    first_keys, first_values = cache(first_partial + handed(given, (1, 0)))
    second_weight = lax.all_gather(
        after(by_far[:, 1], gathered_tokens), ("core", "row"), axis=0, tiled=False
    ).reshape(-1, columns)
    first_sum = attend(
        first_query,
        query_gain[0],
        first_keys,
        first_values,
        live,
        output_weight,
        gate,
    )
    first_sum = jnp.concatenate([first_sum[:, :columns], first_sum[:, columns:]])
    first_sum = first_sum.reshape(tensor_count, -1, columns)
    summed = jnp.sum(exchange(first_sum, "tp").astype(F32), axis=0).astype(BF16)
    summed, second_weight = lax.optimization_barrier((summed, second_weight))
    everywhere = gathered(summed, ("section", "tp"))[:tensor_count]
    everywhere = everywhere.reshape(2, chips * positions, -1).astype(F32)
    everywhere = jnp.concatenate([everywhere[0], everywhere[1]], axis=1)
    first = (state.astype(F32) + everywhere).astype(BF16)

    second_partial, given = projected(gathered_tokens, second_weight)
    given, late = lax.optimization_barrier((given, first))
    second_other = handed(given, (0, 1))
    second_query = to_query(late, query_weight)
    second_keys, second_values = cache(second_partial + second_other)
    second_sum = attend(
        second_query, query_gain[0], second_keys, second_values, live, output_weight, gate
    )
    second_sum = by_index(
        core,
        jnp.stack([second_sum[:, :columns], second_sum[:, columns:]]),
        jnp.stack([second_sum[:, columns:], second_sum[:, :columns]]),
    )
    shape = (cores, tensor_count) + second_sum.shape[1:]
    second_sum = jnp.broadcast_to(second_sum[:, None], shape).reshape((-1,) + shape[2:])
    second_sum = exchange(second_sum, ("core", "tp")).reshape(shape)

    ours, others = first[:, :columns], after(first, second_query)[:, columns:]
    returned = to_other_core(others)
    first = by_index(core, jnp.stack([ours, returned]), jnp.stack([returned, ours]))
    second = (first.astype(F32) + jnp.sum(second_sum.astype(F32), axis=1)).astype(BF16)
    section_out = by_index(section, first, second).reshape(cores, chips, positions, -1)
    section_out = jnp.transpose(section_out, (1, 0, 2, 3)).reshape((1,) + hidden.shape)

    def placed(ours, theirs):
        chosen = by_index(section, ours, theirs).reshape(tensor_count, 2, tokens, head_size)
        return jnp.transpose(chosen, (1, 0, 2, 3)).reshape(1, 1, -1, 1, head_size)

    return (
        placed(first_keys, second_keys),
        placed(first_values, second_values),
        section_out,
    )


def solution(mesh):
    devices = mesh.devices
    fine = Mesh(
        devices.reshape(4, 4, 2, devices.shape[1], devices.shape[2]),
        ("far", "row", "core", "section", "tp"),
    )
    return jax.shard_map(
        body,
        mesh=fine,
        in_specs=(
            P(None, None, SEQ),
            P(SEQ, ("section", "tp"), None),
            P(SEQ),
            P("section", SEQ, "tp", None),
            P("section", None),
            P("section", SEQ, "tp"),
            P("section", None),
            P("section", "tp", SEQ),
            P("section"),
        ),
        out_specs=(
            P("section", SEQ, None, "tp", None),
            P("section", SEQ, None, "tp", None),
            P("section", None, None, SEQ),
        ),
        check_vma=False,
    )
```
